256 devices in a mesh: st: 32 (over y, x, core), gl: 8 (over z).
Axes of the slice: x: 4, y: 4, z: 8, core: 2. Of those that a mesh axis runs over, the one named last changes fastest.
Arguments:
- state_emb: bfloat16 [32768, 512], P(('st', 'gl')), may hold values from -3 to 3
- goal_emb: bfloat16 [32768, 512], P(('gl', 'st')), may hold values from -3 to 3
- positive: int32 [32768], P('st'), may hold values from 0 to 32767, each once
Outputs:
- grad_state: float32 [32768, 512], P(('st', 'gl'))
- grad_goal: float32 [32768, 512], P(('gl', 'st'))
- loss: float32 [], replicated
The draws below stay inside these ranges and needn't reach their ends.
Inputs may be any that keep to these rules, and one draw needn't show every extreme that they name: Every goal is the positive of exactly one state.
All inputs are finite; a program needn't handle non-finite values.
Results may differ from the reference program's by a relative error of at most 0.0016.
Values may be sent and summed in bfloat16 or wider, within the bound.
A program may use at most 64 MiB of HBM per device.

```python
import jax
import jax.numpy as jnp
from jax import lax

E = 512
PAIRS = 32768


def shared_rows(key):
    signs = jnp.where(jax.random.bernoulli(key, 0.5, (3, E)), 1.0, -1.0).astype(jnp.float32)
    third = PAIRS // 3
    copies = max(1, min(16, third - 1))
    offsets = jnp.arange(3, dtype=jnp.int32) * third
    state_rows = jax.random.randint(jax.random.fold_in(key, 11), (3,), 0, max(1, third - 1)) + offsets
    goal_rows = jax.random.randint(jax.random.fold_in(key, 12), (3,), 0, max(1, third - copies)) + offsets
    return (signs, state_rows, goal_rows, copies)


def plant_rows(values, rows, signs, amplitudes, copies):
    targets = [253.0, 250.0, 400.0]
    for index in range(3):
        values = values.at[rows[index]].set(signs[index] * amplitudes[index])
        for step in range(copies):
            offset = 1.0 + 2.0 * step / max(1, copies - 1)
            shrink = 1.0 - offset / targets[index]
            values = values.at[rows[index] + 1 + step].set(signs[index] * amplitudes[index] * shrink)
    return values


def draw_state_emb(key, part):
    signs, state_rows, goal_rows, copies = shared_rows(key)
    key = jax.random.fold_in(key, 1)
    values = jnp.clip(jax.random.normal(key, (PAIRS, E), jnp.float32), -4.0, 4.0) * 0.25
    amplitudes = [1.98, (250.0 / E) ** 0.5, (400.0 / E) ** 0.5]
    values = plant_rows(values, state_rows, signs, amplitudes, 0)
    return values.astype(jnp.bfloat16)


def draw_goal_emb(key, part):
    signs, state_rows, goal_rows, copies = shared_rows(key)
    key = jax.random.fold_in(key, 2)
    values = jnp.clip(jax.random.normal(key, (PAIRS, E), jnp.float32), -4.0, 4.0) * 0.25
    amplitudes = [128.0 / E, (250.0 / E) ** 0.5, (400.0 / E) ** 0.5]
    values = plant_rows(values, goal_rows, signs, amplitudes, copies)
    return values.astype(jnp.bfloat16)


def setup_inputs(seed: int = 0) -> dict:
    arg_keys = jax.random.split(jax.random.key(seed), 4)
    state_emb = draw_state_emb(jax.random.fold_in(arg_keys[3], 71), 0)
    goal_emb = draw_goal_emb(jax.random.fold_in(arg_keys[3], 71), 0)
    positive = jax.random.permutation(arg_keys[2], PAIRS).astype(jnp.int32)
    return dict(state_emb=state_emb, goal_emb=goal_emb, positive=positive)


def reference(state_emb, goal_emb, positive):
    states_all = state_emb.astype(jnp.float32)
    goals_all = goal_emb.astype(jnp.float32)
    block_rows = min(1024, PAIRS)
    block_count = PAIRS // block_rows
    state_blocks = states_all.reshape(block_count, block_rows, E)
    index_blocks = positive.reshape(block_count, block_rows)
    columns = jnp.arange(PAIRS, dtype=jnp.int32)

    def make_logits(state_block):
        return jnp.dot(state_block, goals_all.T, preferred_element_type=jnp.float32, precision=lax.Precision.HIGHEST)

    def first_pass(running, item):
        column_max, column_sum = running
        state_block, index_block = item
        logits = make_logits(state_block)
        row_top = jnp.max(logits, axis=1)
        row_lse = row_top + jnp.log(jnp.sum(jnp.exp(logits - row_top[:, None]), axis=1))
        hits = columns[None, :] == index_block[:, None]
        matched = jnp.sum(jnp.where(hits, logits, jnp.float32(0.0)), axis=1)
        new_max = jnp.maximum(column_max, jnp.max(logits, axis=0))
        column_sum = column_sum * jnp.exp(column_max - new_max) + jnp.sum(jnp.exp(logits - new_max[None, :]), axis=0)
        return (new_max, column_sum), (row_lse, matched)

    start = (jnp.full((PAIRS,), -jnp.inf, jnp.float32), jnp.zeros((PAIRS,), jnp.float32))
    (column_max, column_sum), (row_lse, matched) = lax.scan(first_pass, start, (state_blocks, index_blocks))
    col_lse = column_max + jnp.log(column_sum)
    loss = (jnp.sum(row_lse) + jnp.sum(col_lse) - 2.0 * jnp.sum(matched)) / (2.0 * PAIRS)

    def second_pass(goal_total, item):
        state_block, index_block, lse_block = item
        logits = make_logits(state_block)
        hits = columns[None, :] == index_block[:, None]
        probs = 0.5 * (jnp.exp(logits - lse_block[:, None]) + jnp.exp(logits - col_lse[None, :]))
        weights = (probs - jnp.where(hits, jnp.float32(1.0), jnp.float32(0.0))).astype(jnp.bfloat16)
        weights = lax.optimization_barrier(weights).astype(jnp.float32)
        state_grad = jnp.dot(weights, goals_all, preferred_element_type=jnp.float32, precision=lax.Precision.HIGHEST)
        goal_total = goal_total + jnp.dot(weights.T, state_block, preferred_element_type=jnp.float32, precision=lax.Precision.HIGHEST)
        return goal_total, state_grad

    lse_blocks = row_lse.reshape(block_count, block_rows)
    grad_goal, state_parts = lax.scan(second_pass, jnp.zeros((PAIRS, E), jnp.float32), (state_blocks, index_blocks, lse_blocks))
    grad_state = state_parts.reshape(PAIRS, E)
    return grad_state, grad_goal, loss
```

```python
import functools

import jax
import jax.numpy as jnp
from jax import lax
from jax.experimental import pallas as pl
from jax.experimental.pallas import tpu as pltpu
from jax.sharding import PartitionSpec as P

MESH = pl.DeviceIdType.MESH
LOG2E = 1.4426950408889634
LN2 = 0.6931471805599453
X = 4
Q = X * X
B = 128
E = 512
UNIT = 272
STEP = 32700.0


def quantize(slabs, ref):
    top = slabs[0]
    top = jnp.abs(top)
    for slab in slabs[1:]:
        top = jnp.maximum(top, jnp.abs(slab))
    top = jnp.max(top, axis=0, keepdims=True)
    power = jnp.ceil(jnp.log2(jnp.maximum(top, 1e-30)))
    factor = jnp.exp2(-power) * STEP
    ref[128:144, :] = jnp.broadcast_to(power, (16, 128)).astype(jnp.int32).astype(jnp.int16)
    for slab, start in zip(slabs, (0, 64, 144, 208)):
        codes = jnp.round(slab * factor).astype(jnp.int32)
        ref[start : start + 64, :] = codes.astype(jnp.int16)


def restore(ref, halves=(0, 1)):
    power = ref[128:144, :].astype(jnp.int32).astype(jnp.float32)[0:1, :]
    factor = jnp.exp2(power) * (1.0 / STEP)
    starts = [s for h in halves for s in ((0, 64), (144, 208))[h]]
    return [ref[s : s + 64, :].astype(jnp.int32).astype(jnp.float32) * factor for s in starts]


def combine(parts):
    top = jnp.max(parts, axis=0)
    return top + jnp.log2(jnp.sum(jnp.exp2(parts - top[None]), axis=0))


def kernel(
    Z, state_ref, goal_ref, pos_ref, gs_out, gg_out, loss_out,
    S, G, PS, L, W, St, GS, GG, MR, SR, MC, SC,
    LR, zr_stat, LS, sib_stat, LC, xr_stat, LY, yr_stat, acc,
    ss, sr, zs, zr, xs1, xr1, xs2, xr2, loss_s, loss_r,
    ag_s, ag_r, ga_s, ga_r, sb_s, sb_r, st_s, st_r, rb_s, rb_r, rz_s, rz_r, rx_s, rx_r,
):
    st = lax.axis_index("st")
    z = lax.axis_index("gl")
    c = lax.rem(st, 2)
    chip = st // 2
    x = lax.rem(chip, X)
    y = chip // X
    H = Z // 2
    NB = 2 * Z

    def wrap(v, n):
        return lax.rem(v + n, n)

    def dev(xx, yy, zz, cc):
        return ((yy * X + xx) * 2 + cc, zz)

    sibling = dev(x, y, z, 1 - c)

    def near(axis, k):
        if axis == 0:
            return dev(wrap(x + k, X), y, z, c)
        if axis == 1:
            return dev(x, wrap(y + k, X), z, c)
        return dev(x, y, wrap(z + k, Z), c)

    def rcopy(src, dst, send, recv, to):
        return pltpu.make_async_remote_copy(
            src_ref=src, dst_ref=dst, send_sem=send, recv_sem=recv, device_id=to, device_id_type=MESH
        )

    others = [sibling]
    others += [near(2, k) for k in range(1, Z)]
    others += [near(a, k) for a in (0, 1) for k in range(1, X)]
    barrier = pltpu.get_barrier_semaphore()
    for to in others:
        pl.semaphore_signal(barrier, inc=1, device_id=to, device_id_type=MESH)

    own = c * Z + z
    S[own] = state_ref[...]
    G[chip] = goal_ref[...]
    PS[c] = pos_ref[...]
    pl.semaphore_wait(barrier, len(others))

    def z_copy(s, k):
        block = c * Z + wrap(z - s * (k - 1), Z)
        rows = pl.ds(0, 128) if k < H else (pl.ds(0, 64) if s > 0 else pl.ds(64, 64))
        ref = S.at[block, rows]
        i = 2 * (k - 1) + (s > 0)
        return rcopy(ref, ref, ag_s.at[i], ag_r.at[i], near(2, s))

    def sib_copy(zz):
        ref = S.at[c * Z + zz]
        return rcopy(ref, ref, sb_s.at[zz], sb_r.at[zz], sibling)

    def g_copy(part, phase, o, s, k):
        axis = part if phase == 0 else 1 - part
        back = wrap(-s * (k - 1), X)
        if axis == 0:
            q = wrap(y + o, X) * X + wrap(x + back, X)
        else:
            q = wrap(y + back, X) * X + wrap(x + o, X)
        start = 64 * part
        rows = pl.ds(start, 64) if k == 1 else pl.ds(start + (0 if s > 0 else 32), 32)
        ref = G.at[q, rows]
        i = ((part * 5 + (0 if phase == 0 else 1 + o % X)) * 2 + (k - 1)) * 2 + (s > 0)
        return rcopy(ref, ref, ga_s.at[i], ga_r.at[i], near(axis, s))

    started = []

    def start(copy):
        copy.start()
        started.append(copy)
        return copy

    signs = (1, -1)
    pos_copy = start(rcopy(PS.at[c], PS.at[c], sb_s.at[Z], sb_r.at[Z], sibling))
    zc = {(s, 1): start(z_copy(s, 1)) for s in signs}
    first = {(p, s, 1): start(g_copy(p, 0, 0, s, 1)) for p in (0, 1) for s in signs}
    second = {(p, 0, s, 1): start(g_copy(p, 1, 0, s, 1)) for p in (0, 1) for s in signs}
    sib = [start(sib_copy(z))]

    def first_forward():
        for p in (0, 1):
            for s in signs:
                first[p, s, 1].wait_recv()
                first[p, s, 2] = start(g_copy(p, 0, 0, s, 2))
        for p in (0, 1):
            for o in (1, -1):
                for s in signs:
                    second[p, o, s, 1] = start(g_copy(p, 1, o, s, 1))

    def first_last():
        for p in (0, 1):
            for s in signs:
                first[p, s, 2].wait_recv()
            for s in signs:
                second[p, 2, s, 1] = start(g_copy(p, 1, 2, s, 1))

    def second_forward(o):
        for p in (0, 1):
            for s in signs:
                second[p, o, s, 1].wait_recv()
                second[p, o, s, 2] = start(g_copy(p, 1, o, s, 2))

    def z_forward(k):
        for s in signs:
            zc[s, k - 1].wait_recv()
            zc[s, k] = start(z_copy(s, k))
        for s in signs:
            sib.append(start(sib_copy(wrap(z - s * (k - 1), Z))))

    first_forward()
    for k in range(2, H + 1):
        z_forward(k)
        if k == 2:
            second_forward(0)
            first_last()
        if k == 3:
            second_forward(1)
            second_forward(-1)
        if k == min(4, H):
            second_forward(2)
    for s in signs:
        zc[s, H].wait_recv()
    sib.append(start(sib_copy(wrap(z + H, Z))))
    for o in (0, 1, -1, 2):
        for p in (0, 1):
            for s in signs:
                second[p, o, s, 2].wait_recv()
    pos_copy.wait_recv()
    for copy in sib:
        copy.wait_recv()

    MC[...] = jnp.full(MC.shape, -3e38, jnp.float32)
    SC[...] = jnp.zeros(SC.shape, jnp.float32)

    def first_pass(r, carry):
        left = S[pl.ds(2 * r, 2)].reshape(256, E)

        def logits(k):
            right = G[4 * k : 4 * k + 4].reshape(512, E)
            out = lax.dot_general(
                left, right, (((1,), (1,)), ((), ())), preferred_element_type=jnp.float32
            ) * LOG2E
            L[pl.ds(pl.multiple_of(256 * r, 256), 256), 512 * k : 512 * k + 512] = out
            return out

        row_top = [None] * 8
        row_sum = [None] * 8

        def stats(k, block):
            pieces = [
                [block[32 * i : 32 * i + 32, 128 * j : 128 * j + 128] for j in range(4)] for i in range(8)
            ]
            new_rows = []
            old = MC[:, 512 * k : 512 * k + 512]
            old_top = [old[:, 128 * j : 128 * j + 128] for j in range(4)]
            col_top = list(old_top)
            for i in range(8):
                p = pieces[i]
                best = jnp.maximum(jnp.maximum(p[0], p[1]), jnp.maximum(p[2], p[3]))
                new_rows.append(best if row_top[i] is None else jnp.maximum(row_top[i], best))
                for j in range(4):
                    col_top[j] = jnp.maximum(col_top[j], jnp.max(p[j].reshape(4, 8, 128), axis=0))
            sums = SC[:, 512 * k : 512 * k + 512]
            col_sum = [
                sums[:, 128 * j : 128 * j + 128] * jnp.exp2(old_top[j] - col_top[j]) for j in range(4)
            ]
            for i in range(8):
                p = pieces[i]
                total = None if row_top[i] is None else row_sum[i] * jnp.exp2(row_top[i] - new_rows[i])
                for j in range(4):
                    term = jnp.exp2(p[j] - new_rows[i])
                    total = term if total is None else total + term
                    folded = p[j].reshape(4, 8, 128)
                    col_sum[j] = col_sum[j] + jnp.sum(jnp.exp2(folded - col_top[j][None]), axis=0)
                row_top[i] = new_rows[i]
                row_sum[i] = total
            for j in range(4):
                MC[:, 512 * k + 128 * j : 512 * k + 128 * j + 128] = col_top[j]
                SC[:, 512 * k + 128 * j : 512 * k + 128 * j + 128] = col_sum[j]

        blocks = [logits(0), logits(1)]
        for k in range(4):
            stats(k, blocks[k])
            if k + 2 < 4:
                blocks.append(logits(k + 2))
        for i in range(8):
            at = pl.ds(pl.multiple_of(256 * r + 32 * i, 32), 32)
            MR[at, :] = row_top[i]
            SR[at, :] = row_sum[i]
        return carry

    lax.fori_loop(0, NB // 2, first_pass, 0)

    for q in range(Q):
        m = MC[:, 128 * q : 128 * q + 128]
        top = jnp.max(m, axis=0, keepdims=True)
        total = jnp.sum(SC[:, 128 * q : 128 * q + 128] * jnp.exp2(m - top), axis=0, keepdims=True)
        LC[q : q + 1, :] = top + jnp.log2(total)

    def all_share(axis, n, src, dst, me, base):
        dst[me] = src[...]
        copies = []
        for k in range(1, n):
            i = base + k
            copies.append(start(rcopy(src, dst.at[me], st_s.at[i], st_r.at[i], near(axis, k))))
        return copies

    def arrive(copies):
        for copy in copies:
            copy.wait_recv()

    sx = all_share(0, X, LC, xr_stat, x, 0)

    def lane_combine(b, carry):
        at = pl.ds(pl.multiple_of(128 * b, 128), 128)
        m = MR[at, :].T
        top = jnp.max(m, axis=0, keepdims=True)
        total = jnp.sum(SR[at, :].T * jnp.exp2(m - top), axis=0, keepdims=True)
        LR[pl.ds(b, 1), :] = top + jnp.log2(total)
        return carry

    lax.fori_loop(0, NB, lane_combine, 0)
    sz = all_share(2, Z, LR, zr_stat, z, 16)
    arrive(sx)
    LY[...] = combine(xr_stat[...])
    sy = all_share(1, X, LY, yr_stat, y, 8)

    def transpose_states(b, carry):
        St[:, pl.ds(pl.multiple_of(128 * b, 128), 128)] = S[b].T
        return carry

    lax.fori_loop(0, NB, transpose_states, 0)

    lanes = lax.broadcasted_iota(jnp.int32, (128, 128), 1).astype(jnp.float32)
    first_goal = (z * (2 * Q * B) + c * B).astype(jnp.float32)
    arrive(sz)
    LS[...] = combine(zr_stat[...])
    ssib = start(rcopy(LS, sib_stat, st_s.at[0], st_r.at[0], sibling))

    def spread_positive(b, carry):
        row = PS[b // Z, pl.ds(lax.rem(b, Z), 1), :].astype(jnp.float32)
        at = pl.ds(pl.multiple_of(128 * b, 128), 128)
        SR[at, :] = jnp.broadcast_to(row, (128, 128)).T - lanes - first_goal
        return carry

    lax.fori_loop(0, NB, spread_positive, 0)
    arrive(sy)
    col_lse = combine(yr_stat[...])
    LC2 = col_lse + 1.0
    ssib.wait_recv()
    pair = jnp.stack([LS[...], sib_stat[...]])
    row_lse = combine(pair)
    LY2 = row_lse + 1.0
    zr_stat[0] = LY2

    def spread_rows(b, carry):
        at = pl.ds(pl.multiple_of(128 * b, 128), 128)
        row = zr_stat[0, pl.ds(b, 1), :]
        MR[at, :] = jnp.broadcast_to(row, (128, 128)).T
        return carry

    lax.fori_loop(0, NB, spread_rows, 0)
    xr_stat[0] = LC2
    zr_stat[1] = row_lse
    xr_stat[1] = col_lse
    acc[...] = jnp.zeros(acc.shape, jnp.float32)

    def second_pass(r, carry):
        rows = pl.ds(pl.multiple_of(256 * r, 256), 256)
        out = None
        hit_sum = acc[...]
        for k in range(4):
            for i in range(8):
                at = pl.ds(pl.multiple_of(256 * r + 32 * i, 32), 32)
                rl = MR[at, :]
                pb = SR[at, :]
                for j in range(4):
                    q = 4 * k + j
                    l = L[at, 128 * q : 128 * q + 128]
                    prob = jnp.exp2(l - rl) + jnp.exp2(l - xr_stat[0, q : q + 1, :])
                    hit = pb == jnp.float32(2 * B * q)
                    hit_sum = hit_sum + jnp.sum(jnp.where(hit, l, 0.0).reshape(4, 8, 128), axis=0)
                    W[at, 128 * q : 128 * q + 128] = jnp.where(hit, prob - 1.0, prob).astype(jnp.bfloat16)
            term = jnp.dot(
                W[rows, 512 * k : 512 * k + 512],
                G[4 * k : 4 * k + 4].reshape(512, E),
                preferred_element_type=jnp.float32,
            )
            out = term if out is None else out + term
        acc[...] = hit_sum
        GS[pl.ds(2 * r, 2)] = out.reshape(2, 128, E)
        return carry

    lax.fori_loop(0, NB // 2, second_pass, 0)

    def gs_slabs(b, u):
        return [GS[b, 64 * u : 64 * u + 64, 128 * i : 128 * i + 128] for i in range(4)]

    def rb_copy(zz):
        return rcopy(ss.at[zz], sr.at[zz], rb_s.at[zz], rb_r.at[zz], sibling)

    def give(zz, carry):
        for u in (0, 1):
            quantize(gs_slabs((1 - c) * Z + zz, u), ss.at[zz, u])
        rb_copy(zz).start()
        return carry

    lax.fori_loop(0, Z, give, 0)

    def goal_pass(t, carry):
        at = pl.ds(pl.multiple_of(256 * t, 256), 256)
        out = jnp.dot(St[...], W[:, at], preferred_element_type=jnp.float32)
        GG[2 * t] = out[:, :128]
        GG[2 * t + 1] = out[:, 128:]
        return carry

    lax.fori_loop(0, Q // 2, goal_pass, 0)

    def take(zz, carry):
        rb_copy(zz).wait_recv()
        for u in (0, 1):
            for i, part in enumerate(restore(sr.at[zz, u])):
                GS[c * Z + zz, 64 * u : 64 * u + 64, 128 * i : 128 * i + 128] += part
        return carry

    def rx_copy(p, phase, t, s, k):
        axis = 1 - p if phase == 0 else p
        sg = 0 if s > 0 else 1
        rows = pl.ds(0, UNIT) if k == 1 else (pl.ds(0, 144) if s > 0 else pl.ds(128, 144))
        kind = 0 if k == 2 else 1 + sg
        if phase == 0:
            src, dst = xs1.at[p, t, kind, rows], xr1.at[p, t, sg, k - 1, rows]
            i = ((p * X + t) * 2 + sg) * 2 + (k - 1)
        else:
            src, dst = xs2.at[p, kind, rows], xr2.at[p, sg, k - 1, rows]
            i = 32 + (p * 2 + sg) * 2 + (k - 1)
        return rcopy(src, dst, rx_s.at[i], rx_r.at[i], near(axis, s))

    def chip_at(p, phase, t, d):
        if phase == 0:
            return wrap(y + d, X) * X + t if p == 0 else t * X + wrap(x + d, X)
        return y * X + wrap(x + d, X) if p == 0 else wrap(y + d, X) * X + x

    def gg_slabs(q, p):
        return [GG[q, 256 * p + 64 * i : 256 * p + 64 * i + 64, :] for i in range(4)]

    def bufs(phase, p, t):
        return (xs1.at[p, t], xr1.at[p, t]) if phase == 0 else (xs2.at[p], xr2.at[p])

    def x_open(p, phase, t):
        out, _ = bufs(phase, p, t)
        quantize(gg_slabs(chip_at(p, phase, t, 2), p), out.at[0])
        for s in signs:
            rx_copy(p, phase, t, s, 2).start()

    def x_relay(p, phase, t):
        out, came = bufs(phase, p, t)
        for s in signs:
            sg = 0 if s > 0 else 1
            rx_copy(p, phase, t, s, 2).wait_recv()
            slabs = gg_slabs(chip_at(p, phase, t, s), p)
            for i, part in enumerate(restore(came.at[sg, 1], (sg,))):
                slabs[2 * sg + i] = slabs[2 * sg + i] + part
            quantize(slabs, out.at[1 + sg])
            rx_copy(p, phase, t, s, 1).start()

    def x_close(p, phase, t):
        _, came = bufs(phase, p, t)
        q = chip_at(p, phase, t, 0)
        for s in signs:
            rx_copy(p, phase, t, s, 1).wait_recv()
        for i, (a, b) in enumerate(zip(restore(came.at[0, 0]), restore(came.at[1, 0]))):
            GG[q, 256 * p + 64 * i : 256 * p + 64 * i + 64, :] += a + b

    def x_sent(p, phase, t):
        for s in signs:
            rx_copy(p, phase, t, s, 2).wait_send()
            rx_copy(p, phase, t, s, 1).wait_send()

    def over(step, phase):
        def both(t, carry):
            for p in (0, 1):
                step(p, phase, t)
            return carry

        lax.fori_loop(0, X, both, 0)

    over(x_open, 0)
    lax.fori_loop(0, Z, take, 0)

    def rz_copy(s, u, k):
        sg = 0 if s > 0 else 1
        i = (sg * 2 + u) * H + k - 1
        return rcopy(zs.at[i], zr.at[i], rz_s.at[i], rz_r.at[i], near(2, s))

    def z_step(k):
        for s in signs:
            sg = 0 if s > 0 else 1
            for u in (sg, 1 - sg):
                top = H if u == sg else H - 1
                if k > top:
                    continue
                slabs = gs_slabs(c * Z + wrap(z + s * k, Z), u)
                if k < top:
                    came = rz_copy(s, u, k + 1)
                    came.wait_recv()
                    parts = restore(zr.at[(sg * 2 + u) * H + k])
                    slabs = [a + b for a, b in zip(slabs, parts)]
                quantize(slabs, zs.at[(sg * 2 + u) * H + k - 1])
                rz_copy(s, u, k).start()

    own_rows = zr_stat[1, pl.ds(own, 1), :]
    own_cols = xr_stat[1, pl.ds(chip, 1), :]
    lead = lax.broadcasted_iota(jnp.int32, (8, 128), 0) == 0
    loss_s[0] = jnp.where(lead, own_rows + own_cols, 0.0) - 2.0 * acc[...]

    def loss_share(stage, axis, n):
        copies = []
        for k in range(1, n):
            i = 4 * stage + k if stage < 2 else 8 + k
            copies.append(start(rcopy(loss_s.at[stage], loss_r.at[i], st_s.at[32 + i], st_r.at[32 + i], near(axis, k))))
        return copies

    def loss_add(stage, copies, slots):
        arrive(copies)
        total = loss_s[stage]
        for i in slots:
            total = total + loss_r[i]
        return total

    z_step(H)
    l0 = loss_share(0, 0, X)
    over(x_relay, 0)
    for k in range(H - 1, 0, -1):
        z_step(k)
        if k == H - 1:
            over(x_close, 0)
            for p in (0, 1):
                x_open(p, 1, 0)
            loss_s[1] = loss_add(0, l0, range(1, X))
            l1 = loss_share(1, 1, X)
        if k == max(1, H - 2):
            for p in (0, 1):
                x_relay(p, 1, 0)
            loss_s[2] = loss_add(1, l1, range(5, 4 + X))
            l2 = loss_share(2, 2, Z)
    for p in (0, 1):
        x_close(p, 1, 0)
    loss_s[3] = loss_add(2, l2, range(9, 8 + Z))
    l3 = start(rcopy(loss_s.at[3], loss_r.at[0], st_s.at[32], st_r.at[32], sibling))
    gg_out[...] = GG[chip].T
    for s in signs:
        sg = 0 if s > 0 else 1
        for u in (0, 1):
            rz_copy(s, u, 1).wait_recv()
            for i, part in enumerate(restore(zr.at[(sg * 2 + u) * H])):
                GS[own, 64 * u : 64 * u + 64, 128 * i : 128 * i + 128] += part
    gs_out[...] = GS[own]
    total = loss_add(3, [l3], [0])
    loss_out[0, 0] = jnp.sum(total) * (LN2 / (4.0 * Q * Z * B))

    for copy in started:
        copy.wait_send()

    def given(zz, carry):
        rb_copy(zz).wait_send()
        return carry

    lax.fori_loop(0, Z, given, 0)
    over(x_sent, 0)
    for p in (0, 1):
        x_sent(p, 1, 0)
    for s in signs:
        sg = 0 if s > 0 else 1
        for u in (0, 1):
            for k in range(1, (H if u == sg else H - 1) + 1):
                rz_copy(s, u, k).wait_send()


def body(state_emb, goal_emb, positive):
    Z = lax.axis_size("gl")
    H = Z // 2
    NB = 2 * Z
    R, C = NB * B, Q * B
    vmem = pltpu.VMEM
    f32, bf16, i16 = jnp.float32, jnp.bfloat16, jnp.int16
    dma = pltpu.SemaphoreType.DMA
    scratch = [
        vmem((NB, B, E), bf16), vmem((Q, B, E), bf16), vmem((2, Z, B), jnp.int32),
        vmem((R, C), f32), vmem((R, C), bf16), vmem((E, R), bf16),
        vmem((NB, B, E), f32), vmem((Q, E, B), f32),
        vmem((R, B), f32), vmem((R, B), f32), vmem((8, C), f32), vmem((8, C), f32),
        vmem((NB, B), f32), vmem((Z, NB, B), f32), vmem((NB, B), f32), vmem((NB, B), f32),
        vmem((Q, B), f32), vmem((X, Q, B), f32), vmem((Q, B), f32), vmem((X, Q, B), f32),
        vmem((8, B), f32),
        vmem((Z, 2, UNIT, B), i16), vmem((Z, 2, UNIT, B), i16),
        vmem((4 * H, UNIT, B), i16), vmem((4 * H, UNIT, B), i16),
        vmem((2, X, 3, UNIT, B), i16), vmem((2, X, 2, 2, UNIT, B), i16),
        vmem((2, 3, UNIT, B), i16), vmem((2, 2, 2, UNIT, B), i16),
        vmem((4, 8, B), f32), vmem((8 + Z, 8, B), f32),
        dma((2 * H,)), dma((2 * H,)), dma((40,)), dma((40,)), dma((Z + 1,)), dma((Z + 1,)),
        dma((48,)), dma((48,)), dma((Z,)), dma((Z,)), dma((4 * H,)), dma((4 * H,)),
        dma((40,)), dma((40,)),
    ]
    whole = pl.BlockSpec(memory_space=pltpu.VMEM)
    grad_state, grad_goal, loss = pl.pallas_call(
        functools.partial(kernel, Z),
        out_shape=(
            jax.ShapeDtypeStruct((B, E), f32),
            jax.ShapeDtypeStruct((B, E), f32),
            jax.ShapeDtypeStruct((1, 1), f32),
        ),
        in_specs=[whole] * 3,
        out_specs=(whole, whole, pl.BlockSpec(memory_space=pltpu.SMEM)),
        scratch_shapes=scratch,
        compiler_params=pltpu.CompilerParams(
            collective_id=0, has_side_effects=True, vmem_limit_bytes=62 * 1024 * 1024
        ),
    )(state_emb, goal_emb, positive.reshape(Z, B))
    return grad_state, grad_goal, loss.reshape(())


def solution(mesh):
    return jax.shard_map(
        body,
        mesh=mesh,
        in_specs=(P(("st", "gl"), None), P(("gl", "st"), None), P("st")),
        out_specs=(P(("st", "gl"), None), P(("gl", "st"), None), P()),
        check_vma=False,
    )
```

```python
import functools

import jax
import jax.numpy as jnp
from jax import lax
from jax.experimental import pallas as pl
from jax.experimental.pallas import tpu as pltpu
from jax.sharding import PartitionSpec as P

MESH = pl.DeviceIdType.MESH
LOG2E = 1.4426950408889634
LN2 = 0.6931471805599453
X = 4
Q = X * X
B = 128
E = 512
UNIT = 272
STEP = 32700.0


def quantize_all(items):
    tops = []
    for slabs, _ in items:
        top = jnp.abs(slabs[0])
        for slab in slabs[1:]:
            top = jnp.maximum(top, jnp.abs(slab))
        tops.append(jnp.max(top, axis=0, keepdims=True))
    powers = [jnp.ceil(jnp.log2(jnp.maximum(top, 1e-30))) for top in tops]
    factors = [jnp.exp2(-power) * STEP for power in powers]
    for (slabs, ref), power, factor in zip(items, powers, factors):
        ref[128:144, :] = jnp.broadcast_to(power, (16, 128)).astype(jnp.int32).astype(jnp.int16)
        for slab, start in zip(slabs, (0, 64, 144, 208)):
            ref[start : start + 64, :] = jnp.round(slab * factor).astype(jnp.int32).astype(jnp.int16)


def restore(ref):
    power = ref[128:144, :].astype(jnp.int32).astype(jnp.float32)[0:1, :]
    factor = jnp.exp2(power) * (1.0 / STEP)
    return [ref[s : s + 64, :].astype(jnp.int32).astype(jnp.float32) * factor for s in (0, 64, 144, 208)]


def combine(parts):
    top = jnp.max(parts, axis=0)
    return top + jnp.log2(jnp.sum(jnp.exp2(parts - top[None]), axis=0))


def kernel(
    Z, state_ref, goal_ref, pos_ref, gs_out, gg_out, loss_out,
    S, G, PS, L, W0, W1, St0, St1, GS, GR, GG, MR, SR, PB, MC, SC,
    LR, zr_stat, LS, sib_stat, LC, xr_stat, LY, yr_stat, acc,
    zs, zr, s1, r1, s2, r2, loss_s, loss_r, out_goal,
    in_sem, ag_s, ag_r, gf_s, gf_r, gg_s, gg_r, sb_s, sb_r, st_s, st_r, rb_s, rb_r, rz_s, rz_r,
    g1_s, g1_r, g2_s, g2_r,
):
    st = lax.axis_index("st")
    z = lax.axis_index("gl")
    c = lax.rem(st, 2)
    chip = st // 2
    x = lax.rem(chip, X)
    y = chip // X
    H = Z // 2
    NB = 2 * Z

    def wrap(v, n):
        return lax.rem(v + n, n)

    def dev(xx, yy, zz, cc):
        return ((yy * X + xx) * 2 + cc, zz)

    sibling = dev(x, y, z, 1 - c)

    f = x + c * (y - x)
    g = y + c * (x - y)

    def near(axis, k):
        if axis == "z":
            return dev(x, y, wrap(z + k, Z), c)
        ff, gg = (wrap(f + k, X), g) if axis == "f" else (f, wrap(g + k, X))
        return dev(ff + c * (gg - ff), gg + c * (ff - gg), z, c)

    def rcopy(src, dst, send, recv, to):
        return pltpu.make_async_remote_copy(
            src_ref=src, dst_ref=dst, send_sem=send, recv_sem=recv, device_id=to, device_id_type=MESH
        )

    others = [sibling]
    others += [near("z", k) for k in range(1, Z)]
    others += [near(a, k) for a in "fg" for k in range(1, X)]
    barrier = pltpu.get_barrier_semaphore()
    for to in others:
        pl.semaphore_signal(barrier, inc=1, device_id=to, device_id_type=MESH)

    home = X * f + g
    loads = [
        pltpu.make_async_copy(state_ref, S.at[c, z], in_sem.at[0]),
        pltpu.make_async_copy(goal_ref, G.at[home], in_sem.at[1]),
        pltpu.make_async_copy(pos_ref, PS.at[c], in_sem.at[2]),
    ]
    for copy in loads:
        copy.start()
    for copy in loads:
        copy.wait()
    pl.semaphore_wait(barrier, len(others))

    started = []

    def start(make, *args):
        make(*args).start()
        started.append((make, args))

    signs = (1, -1)

    def z_copy(s, k, half):
        rows = pl.ds(64 * half, 64)
        ref = S.at[c, wrap(z - s * (k - 1), Z), rows]
        i = (2 * (k - 1) + (s > 0)) * 2 + half
        return rcopy(ref, ref, ag_s.at[i], ag_r.at[i], near("z", s))

    def sib_copy(d):
        zz = wrap(z + d, Z)
        ref = S.at[c, zz]
        return rcopy(ref, ref, sb_s.at[zz], sb_r.at[zz], sibling)

    def pos_copy():
        return rcopy(PS.at[c], PS.at[c], sb_s.at[Z], sb_r.at[Z], sibling)

    def f_copy(k):
        ref = G.at[home]
        return rcopy(ref, ref, gf_s.at[k - 1], gf_r.at[k - 1], near("f", k))

    def g_copy(o, k):
        ref = G.at[X * wrap(f + o, X) + g]
        i = 3 * o + k - 1
        return rcopy(ref, ref, gg_s.at[i], gg_r.at[i], near("g", k))

    def z_piece(k, half, s):
        if k > 1:
            z_copy(s, k - 1, half).wait_recv()
        if k < H or half == (s < 0):
            start(z_copy, s, k, half)

    def z_forward(k):
        for late in (0, 1):
            for s in signs:
                z_piece(k, late ^ int(s < 0), s)
        for s in signs:
            start(sib_copy, -s * (k - 1))

    near_first = (1, 3, 2)
    for k in near_first:
        start(f_copy, k)
    for s in signs:
        z_piece(1, int(s < 0), s)
    start(pos_copy)
    MC[...] = jnp.full(MC.shape, -3e38, jnp.float32)
    SC[...] = jnp.zeros(SC.shape, jnp.float32)
    MR[...] = jnp.full(MR.shape, -3e38, jnp.float32)
    for s in signs:
        z_piece(1, int(s > 0), s)
    SR[...] = jnp.zeros(SR.shape, jnp.float32)
    for k in near_first:
        start(g_copy, 0, k)
    start(sib_copy, 0)
    for n, o in enumerate((3, 1, 2)):
        f_copy(near_first[n]).wait_recv()
        for k in near_first:
            start(g_copy, o, k)
        if n == 1:
            z_forward(2)

    lanes = lax.broadcasted_iota(jnp.int32, (128, 128), 1).astype(jnp.float32)
    first_goal = (z * (2 * Q * B) + c * B).astype(jnp.float32)
    pos_copy().wait_recv()

    def spread_positive(b, carry):
        row = PS[b // Z, pl.ds(lax.rem(b, Z), 1), :].astype(jnp.float32)
        at = pl.ds(pl.multiple_of(128 * b, 128), 128)
        PB[at, :] = jnp.broadcast_to(row, (128, 128)).T - lanes - first_goal
        return carry

    lax.fori_loop(0, NB, spread_positive, 0)

    def goals_in(o):
        for k in near_first:
            g_copy(o, k).wait_recv()

    def states_in(ds):
        for d in ds:
            sib_copy(d).wait_recv()

    def unit_logits(zz, ff):
        left = S[:, pl.ds(zz, 1)].reshape(256, E)
        right = G[pl.ds(X * ff, X)].reshape(512, E)
        return lax.dot_general(left, right, (((1,), (1,)), ((), ())), preferred_element_type=jnp.float32)

    def unit_stats(zz, ff, block):
        cols = pl.ds(pl.multiple_of(512 * ff, 512), 512)
        old = MC[:, cols]
        old_top = [old[:, 128 * j : 128 * j + 128] for j in range(4)]
        col_top = list(old_top)
        pieces, rows, new_rows = [], [], []
        for i in range(8):
            at = pl.ds(pl.multiple_of((i // 4 * Z + zz) * 128 + 32 * (i % 4), 32), 32)
            rows.append(at)
            part = block[32 * i : 32 * i + 32] * LOG2E
            L[at, cols] = part
            p = [part[:, 128 * j : 128 * j + 128] for j in range(4)]
            pieces.append(p)
            best = jnp.maximum(jnp.maximum(p[0], p[1]), jnp.maximum(p[2], p[3]))
            new_rows.append(jnp.maximum(MR[at, :], best))
            for j in range(4):
                col_top[j] = jnp.maximum(col_top[j], jnp.max(p[j].reshape(4, 8, 128), axis=0))
        sums = SC[:, cols]
        col_sum = [sums[:, 128 * j : 128 * j + 128] * jnp.exp2(old_top[j] - col_top[j]) for j in range(4)]
        for i in range(8):
            p = pieces[i]
            total = SR[rows[i], :] * jnp.exp2(MR[rows[i], :] - new_rows[i])
            for j in range(4):
                total = total + jnp.exp2(p[j] - new_rows[i])
                folded = p[j].reshape(4, 8, 128)
                col_sum[j] = col_sum[j] + jnp.sum(jnp.exp2(folded - col_top[j][None]), axis=0)
            MR[rows[i], :] = new_rows[i]
            SR[rows[i], :] = total
        MC[:, cols] = jnp.concatenate(col_top, axis=1)
        SC[:, cols] = jnp.concatenate(col_sum, axis=1)

    steps = (
        ((0, 0), (1, 0), (2, 0), (3, 0)),
        ((0, 3), (1, 3), (2, 3), (3, 3)),
        ((4, 0), (4, 3), (0, 1), (1, 1)),
        ((2, 1), (3, 1), (4, 1), (5, 0)),
        ((5, 3), (5, 1), (6, 0), (6, 3)),
        ((6, 1), (0, 2), (1, 2), (2, 2)),
        ((3, 2), (4, 2), (5, 2), (6, 2)),
        ((7, 0), (7, 3), (7, 1), (7, 2)),
    )

    def step(i, carry):
        @pl.when(i == 0)
        def _():
            goals_in(0)
            z_forward(3)
            states_in((0, 1, -1, 2))

        @pl.when(i == 1)
        def _():
            goals_in(3)

        @pl.when(i == 2)
        def _():
            goals_in(1)
            states_in((-2,))

        @pl.when(i == 3)
        def _():
            z_forward(4)
            states_in((3,))

        @pl.when(i == 4)
        def _():
            states_in((-3,))

        @pl.when(i == 5)
        def _():
            for s in signs:
                z_copy(s, H, int(s < 0)).wait_recv()
            start(sib_copy, H)
            goals_in(2)

        @pl.when(i == 7)
        def _():
            states_in((H,))

        places = []
        for j in range(4):
            n = sum(steps[m][j][0] << (3 * m) for m in range(8))
            o = sum(steps[m][j][1] << (2 * m) for m in range(8))
            n = lax.rem(jnp.right_shift(n, 3 * i), 8)
            o = lax.rem(jnp.right_shift(o, 2 * i), 4)
            away = (n + 1) // 2 * (2 * lax.rem(n, 2) - 1)
            places.append((wrap(z + away, Z), wrap(f + o, X)))
        blocks = [unit_logits(*places[0])]
        for j in range(4):
            if j < 3:
                blocks.append(unit_logits(*places[j + 1]))
            unit_stats(*places[j], blocks[j])
        return carry

    lax.fori_loop(0, 8, step, 0)

    for q in range(Q):
        m = MC[:, 128 * q : 128 * q + 128]
        top = jnp.max(m, axis=0, keepdims=True)
        total = jnp.sum(SC[:, 128 * q : 128 * q + 128] * jnp.exp2(m - top), axis=0, keepdims=True)
        LC[q : q + 1, :] = top + jnp.log2(total)

    def share_copy(axis, src, dst, me, base, k):
        return rcopy(src, dst.at[me], st_s.at[base + k], st_r.at[base + k], near(axis, k))

    def all_share(axis, n, src, dst, me, base):
        dst[me] = src[...]
        for k in range(1, n):
            start(share_copy, axis, src, dst, me, base, k)
        return [share_copy(axis, src, dst, me, base, k) for k in range(1, n)]

    def arrive(copies):
        for copy in copies:
            copy.wait_recv()

    sx = all_share("f", X, LC, xr_stat, f, 0)

    def lane_combine(b, carry):
        at = pl.ds(pl.multiple_of(128 * b, 128), 128)
        m = MR[at, :].T
        top = jnp.max(m, axis=0, keepdims=True)
        total = jnp.sum(SR[at, :].T * jnp.exp2(m - top), axis=0, keepdims=True)
        LR[pl.ds(b, 1), :] = top + jnp.log2(total)
        return carry

    lax.fori_loop(0, NB, lane_combine, 0)
    sz = all_share("z", Z, LR, zr_stat, z, 16)
    arrive(sx)
    LY[...] = combine(xr_stat[...])
    sy = all_share("g", X, LY, yr_stat, g, 8)

    def chunk_block(i, odd):
        pair = lax.rem(z // 2 + H // 2 + (1 + lax.rem(i, 2) if odd else 3 * lax.rem(i, 2)), H)
        late = i // 2
        return ((1 - c) * (1 - late) + c * late) * Z + 2 * pair

    def transpose_states(i, carry):
        for odd, out in ((0, St0), (1, St1)):
            b = chunk_block(i, odd)
            out[:, pl.ds(pl.multiple_of(256 * i, 256), 256)] = (
                S[b // Z, pl.ds(lax.rem(b, Z), 2)].reshape(256, E).T
            )
        return carry

    lax.fori_loop(0, 4, transpose_states, 0)

    arrive(sz)
    LS[...] = combine(zr_stat[...])
    def ls_copy():
        return rcopy(LS, sib_stat, st_s.at[0], st_r.at[0], sibling)

    start(ls_copy)
    arrive(sy)
    col_lse = combine(yr_stat[...])
    LC2 = col_lse + 1.0
    ls_copy().wait_recv()
    pair = jnp.stack([LS[...], sib_stat[...]])
    row_lse = combine(pair)
    LY2 = row_lse + 1.0
    zr_stat[0] = LY2

    xr_stat[0] = LC2
    loss_s[0] = ((row_lse + col_lse)[:8] + (row_lse + col_lse)[8:]) * (1.0 / NB)
    acc[...] = jnp.zeros(acc.shape, jnp.float32)

    def weights(b, out_ref, i):
        for n in (0, 1):
            at = pl.ds(pl.multiple_of(128 * (b + n), 128), 128)
            MR[at, :] = jnp.broadcast_to(zr_stat[0, pl.ds(b + n, 1), :], (128, 128)).T
        hit_sum = acc[...]
        marks = [(256 * (c * q + (1 - c) * (q % X * X + q // X))).astype(jnp.float32) for q in range(Q)]
        for n in range(8):
            at = pl.ds(pl.multiple_of(128 * b + 32 * n, 32), 32)
            rl = MR[at, :]
            pb = PB[at, :]
            for q in range(Q):
                l = L[at, 128 * q : 128 * q + 128]
                prob = jnp.exp2(l - rl) + jnp.exp2(l - xr_stat[0, q : q + 1, :])
                hit = pb == marks[q]
                hit_sum = hit_sum + jnp.sum(jnp.where(hit, l, 0.0).reshape(4, 8, 128), axis=0)
                out_ref[i, 32 * n : 32 * n + 32, 128 * q : 128 * q + 128] = jnp.where(
                    hit, prob - 1.0, prob
                ).astype(jnp.bfloat16)
        acc[...] = hit_sum

    def state_part(b, w_ref, i):
        out = jnp.dot(w_ref[i], G[...].reshape(Q * B, E), preferred_element_type=jnp.float32)
        GS[pl.ds(b, 2)] = out.reshape(2, 128, E)

    def rb_copy(i, odd):
        b = chunk_block(i, odd)
        pair = lax.rem(b, Z) // 2
        return rcopy(
            GS.at[pl.ds(b, 2)], GR.at[pl.ds(2 * pair, 2)], rb_s.at[2 * i + odd], rb_r.at[2 * i + odd], sibling
        )

    def rz_copy(s, u, k):
        sg = 0 if s > 0 else 1
        i = (sg * 2 + u) * H + k - 1
        return rcopy(zs.at[i], zr.at[i], rz_s.at[i], rz_r.at[i], near("z", s))

    def gs_slabs(zz, u):
        rows = pl.ds(64 * u, 64)
        return [
            GS[c * Z + zz, rows, 128 * i : 128 * i + 128] + GR[zz, rows, 128 * i : 128 * i + 128]
            for i in range(4)
        ]

    def z_step(k):
        items = [(s, u) for s in signs for u in (0, 1) if k <= (H if u == (s < 0) else H - 1)]
        ready = []
        for s, u in items:
            if k < (H if u == (s < 0) else H - 1):
                rz_copy(s, u, k + 1).wait_recv()
        for s, u in items:
            at = ((0 if s > 0 else 1) * 2 + u) * H + k
            slabs = gs_slabs(wrap(z + s * k, Z), u)
            if k < (H if u == (s < 0) else H - 1):
                slabs = [a + b for a, b in zip(slabs, restore(zr.at[at]))]
            ready.append((slabs, zs.at[at - 1]))
        quantize_all(ready)
        for s, u in items:
            rz_copy(s, u, k).start()

    weights(chunk_block(0, 0), W0, 0)

    def second_pass(i, carry):
        b0, b1 = chunk_block(i, 0), chunk_block(i, 1)
        weights(b1, W1, i)
        state_part(b0, W0, i)
        ahead = jnp.minimum(i + 1, 3)

        @pl.when(i < 2)
        def _():
            rb_copy(i, 0).start()

        @pl.when(i == 2)
        def _():
            rb_copy(0, 0).wait_recv()
            z_step(H)

        @pl.when(i < 3)
        def _():
            weights(chunk_block(ahead, 0), W0, ahead)
            state_part(b1, W1, i)

        @pl.when(i == 3)
        def _():
            state_part(b1, W1, i)

        @pl.when(i < 2)
        def _():
            rb_copy(i, 1).start()

        return carry

    lax.fori_loop(0, 4, second_pass, 0)
    for i, odd in ((0, 1), (1, 0), (1, 1)):
        rb_copy(i, odd).wait_recv()

    loss_s[0] = loss_s[0] - 2.0 * acc[...]

    def loss_copy(stage, axis, k):
        i = 4 * stage + k if stage < 2 else 8 + k
        return rcopy(loss_s.at[stage], loss_r.at[i], st_s.at[32 + i], st_r.at[32 + i], near(axis, k))

    def loss_share(stage, axis, n):
        for k in range(1, n):
            start(loss_copy, stage, axis, k)
        return [loss_copy(stage, axis, k) for k in range(1, n)]

    def loss_add(stage, copies, slots):
        arrive(copies)
        total = loss_s[stage]
        for i in slots:
            total = total + loss_r[i]
        return total

    l0 = loss_share(0, "f", X)

    def p1_copy(k, h):
        i = 2 * (k - 1) + h
        return rcopy(
            s1.at[k, pl.ds(2 * h, 2)], r1.at[k - 1, pl.ds(2 * h, 2)], g1_s.at[i], g1_r.at[i], near("f", k)
        )

    def halves(out):
        return [[out[256 * u + 64 * i : 256 * u + 64 * i + 64, :] for i in range(4)] for u in (0, 1)]

    def goal_pass(i, carry):
        k = lax.rem(jnp.right_shift(54, 2 * i), 4)
        ff = wrap(f + k, X)
        ready = []
        for h in (0, 1):
            at = pl.ds(pl.multiple_of((X * ff + 2 * h) * 128, 256), 256)
            out = jnp.dot(St0[...], W0[:, :, at].reshape(1024, 256), preferred_element_type=jnp.float32)
            out = out + jnp.dot(St1[...], W1[:, :, at].reshape(1024, 256), preferred_element_type=jnp.float32)
            for j in (0, 1):
                block = out[:, 128 * j : 128 * j + 128]
                GG[X * ff + 2 * h + j] = block
                for u, slabs in enumerate(halves(block)):
                    ready.append((slabs, s1.at[k, 2 * h + j, u]))
            quantize_all(ready[4 * h :])

            @pl.when(i < 3)
            def _():
                p1_copy(k, h).start()

        @pl.when(i == 0)
        def _():
            z_step(H - 1)

        @pl.when(i == 3)
        def _():
            z_step(H - 2)

        return carry

    lax.fori_loop(0, X, goal_pass, 0)
    loss_s[1] = loss_add(0, l0, range(1, X))
    l1 = loss_share(1, "g", X)

    def p2_copy(k):
        return rcopy(s2.at[k - 1], r2.at[k - 1], g2_s.at[k - 1], g2_r.at[k - 1], near("g", k))

    def summed(gg):
        blocks = halves(GG[X * f + gg])
        for k in (2, 1, 3):
            for u in (0, 1):
                blocks[u] = [a + b for a, b in zip(blocks[u], restore(r1.at[k - 1, gg, u]))]
        return blocks

    for k in (2, 1):
        for h in (0, 1):
            p1_copy(k, h).wait_recv()
    loss_s[2] = loss_add(1, l1, range(5, 4 + X))
    l2 = loss_share(2, "z", Z)
    z_step(1)
    for h in (0, 1):
        p1_copy(3, h).wait_recv()
    for k in (2, 1, 3):
        quantize_all([(slabs, s2.at[k - 1, u]) for u, slabs in enumerate(summed(wrap(g + k, X)))])
        p2_copy(k).start()
    mine = summed(g)
    loss_s[3] = loss_add(2, l2, range(9, 8 + Z))

    def loss_last():
        return rcopy(loss_s.at[3], loss_r.at[0], st_s.at[32], st_r.at[32], sibling)

    start(loss_last)
    for u in (0, 1):
        slabs = gs_slabs(z, u)
        for s in signs:
            rz_copy(s, u, 1).wait_recv()
            slabs = [a + b for a, b in zip(slabs, restore(zr.at[((0 if s > 0 else 1) * 2 + u) * H]))]
        for i, part in enumerate(slabs):
            GS[c * Z + z, 64 * u : 64 * u + 64, 128 * i : 128 * i + 128] = part
    gs_store = pltpu.make_async_copy(GS.at[c * Z + z], gs_out, in_sem.at[0])
    gs_store.start()
    for k in (1, 3, 2):
        p2_copy(k).wait_recv()
        for u in (0, 1):
            mine[u] = [a + b for a, b in zip(mine[u], restore(r2.at[k - 1, u]))]
    for u in (0, 1):
        for i, part in enumerate(mine[u]):
            GG[home, 256 * u + 64 * i : 256 * u + 64 * i + 64, :] = part
    out_goal[...] = GG[home].T
    gg_store = pltpu.make_async_copy(out_goal, gg_out, in_sem.at[1])
    gg_store.start()
    total = loss_add(3, [loss_last()], [0])
    loss_out[0, 0] = jnp.sum(total) * (LN2 / (4.0 * Q * Z * B))

    for make, args in started:
        make(*args).wait_send()
    for i in (0, 1):
        for odd in (0, 1):
            rb_copy(i, odd).wait_send()
    for k in range(1, X):
        for h in (0, 1):
            p1_copy(k, h).wait_send()
        p2_copy(k).wait_send()
    for s in signs:
        for u in (0, 1):
            for k in range(1, (H if u == (s < 0) else H - 1) + 1):
                rz_copy(s, u, k).wait_send()
    gs_store.wait()
    gg_store.wait()


def hand_over(gs_in, gg_in, loss_in, gs_out, gg_out, loss_out):
    gs_out[...] = gs_in[...]
    gg_out[...] = gg_in[...]
    loss_out[0, 0] = loss_in[0, 0]


def body(state_emb, goal_emb, positive):
    Z = lax.axis_size("gl")
    H = Z // 2
    NB = 2 * Z
    R, C = NB * B, Q * B
    vmem = pltpu.VMEM
    f32, bf16, i16 = jnp.float32, jnp.bfloat16, jnp.int16
    dma = pltpu.SemaphoreType.DMA
    scratch = [
        vmem((2, Z, B, E), bf16), vmem((Q, B, E), bf16), vmem((2, Z, B), jnp.int32),
        vmem((R, C), f32), vmem((4, 256, C), bf16), vmem((4, 256, C), bf16),
        vmem((E, R // 2), bf16), vmem((E, R // 2), bf16),
        vmem((NB, B, E), f32), vmem((Z, B, E), f32), vmem((Q, E, B), f32),
        vmem((R, B), f32), vmem((R, B), f32), vmem((R, B), f32), vmem((8, C), f32), vmem((8, C), f32),
        vmem((NB, B), f32), vmem((Z, NB, B), f32), vmem((NB, B), f32), vmem((NB, B), f32),
        vmem((Q, B), f32), vmem((X, Q, B), f32), vmem((Q, B), f32), vmem((X, Q, B), f32),
        vmem((8, B), f32),
        vmem((4 * H, UNIT, B), i16), vmem((4 * H, UNIT, B), i16),
        vmem((X, X, 2, UNIT, B), i16), vmem((X - 1, X, 2, UNIT, B), i16),
        vmem((X - 1, 2, UNIT, B), i16), vmem((X - 1, 2, UNIT, B), i16),
        vmem((4, 8, B), f32), vmem((8 + Z, 8, B), f32), vmem((B, E), f32),
        dma((3,)), dma((4 * H,)), dma((4 * H,)), dma((3,)), dma((3,)), dma((12,)), dma((12,)),
        dma((Z + 1,)), dma((Z + 1,)), dma((48,)), dma((48,)), dma((4,)), dma((4,)),
        dma((4 * H,)), dma((4 * H,)), dma((6,)), dma((6,)), dma((3,)), dma((3,)),
    ]
    there = pl.BlockSpec(memory_space=pl.ANY)
    whole = pl.BlockSpec(memory_space=pltpu.VMEM)
    scalar = pl.BlockSpec(memory_space=pltpu.SMEM)
    shapes = (
        jax.ShapeDtypeStruct((B, E), f32),
        jax.ShapeDtypeStruct((B, E), f32),
        jax.ShapeDtypeStruct((1, 1), f32),
    )
    results = pl.pallas_call(
        functools.partial(kernel, Z),
        out_shape=shapes,
        in_specs=[there] * 3,
        out_specs=(there, there, scalar),
        scratch_shapes=scratch,
        compiler_params=pltpu.CompilerParams(
            collective_id=0, has_side_effects=True, vmem_limit_bytes=62 * 1024 * 1024
        ),
    )(state_emb, goal_emb, positive.reshape(Z, B))
    grad_state, grad_goal, loss = pl.pallas_call(
        hand_over,
        out_shape=shapes,
        in_specs=[whole, whole, scalar],
        out_specs=(whole, whole, scalar),
    )(*results)
    return grad_state, grad_goal, loss.reshape(())


def solution(mesh):
    return jax.shard_map(
        body,
        mesh=mesh,
        in_specs=(P(("st", "gl"), None), P(("gl", "st"), None), P("st")),
        out_specs=(P(("st", "gl"), None), P(("gl", "st"), None), P()),
        check_vma=False,
    )
```

```python
import functools

import jax
import jax.numpy as jnp
from jax import lax
from jax.experimental import pallas as pl
from jax.experimental.pallas import tpu as pltpu
from jax.sharding import PartitionSpec as P

MESH = pl.DeviceIdType.MESH
LOG2E = 1.4426950408889634
LN2 = 0.6931471805599453
X = 4
Q = X * X
B = 128
E = 512
UNIT = 272
STEP = 32700.0


def quantize_all(items):
    tops = []
    for slabs, _ in items:
        top = jnp.abs(slabs[0])
        for slab in slabs[1:]:
            top = jnp.maximum(top, jnp.abs(slab))
        tops.append(jnp.max(top, axis=0, keepdims=True))
    powers = [jnp.ceil(jnp.log2(jnp.maximum(top, 1e-30))) for top in tops]
    factors = [jnp.exp2(-power) * STEP for power in powers]
    for (slabs, ref), power, factor in zip(items, powers, factors):
        ref[128:144, :] = jnp.broadcast_to(power, (16, 128)).astype(jnp.int32).astype(jnp.int16)
        for slab, start in zip(slabs, (0, 64, 144, 208)):
            ref[start : start + 64, :] = jnp.round(slab * factor).astype(jnp.int32).astype(jnp.int16)


def restore(ref):
    power = ref[128:144, :].astype(jnp.int32).astype(jnp.float32)[0:1, :]
    factor = jnp.exp2(power) * (1.0 / STEP)
    return [ref[s : s + 64, :].astype(jnp.int32).astype(jnp.float32) * factor for s in (0, 64, 144, 208)]


def combine(parts):
    top = jnp.max(parts, axis=0)
    return top + jnp.log2(jnp.sum(jnp.exp2(parts - top[None]), axis=0))


def kernel(
    Z, state_ref, goal_ref, pos_ref, gs_out, gg_out, loss_out,
    S, G, PS, L, W0, W1, St, GS, GR, GG, MR, SR, PB, MC, SC,
    LR, zr_stat, LS, sib_stat, LC, xr_stat, LY, yr_stat, acc,
    zs, zr, s1, r1, s2, r2, loss_s, loss_r, out_goal,
    in_sem, ag_s, ag_r, gf_s, gf_r, gg_s, gg_r, sb_s, sb_r, st_s, st_r, rb_s, rb_r, rz_s, rz_r,
    g1_s, g1_r, g2_s, g2_r,
):
    st = lax.axis_index("st")
    z = lax.axis_index("gl")
    c = lax.rem(st, 2)
    chip = st // 2
    x = lax.rem(chip, X)
    y = chip // X
    H = Z // 2
    NB = 2 * Z

    def wrap(v, n):
        return lax.rem(v + n, n)

    def dev(xx, yy, zz, cc):
        return ((yy * X + xx) * 2 + cc, zz)

    sibling = dev(x, y, z, 1 - c)

    f = x + c * (y - x)
    g = y + c * (x - y)

    def near(axis, k):
        if axis == "z":
            return dev(x, y, wrap(z + k, Z), c)
        ff, gg = (wrap(f + k, X), g) if axis == "f" else (f, wrap(g + k, X))
        return dev(ff + c * (gg - ff), gg + c * (ff - gg), z, c)

    def rcopy(src, dst, send, recv, to):
        return pltpu.make_async_remote_copy(
            src_ref=src, dst_ref=dst, send_sem=send, recv_sem=recv, device_id=to, device_id_type=MESH
        )

    others = [sibling]
    others += [near("z", k) for k in range(1, Z)]
    others += [near(a, k) for a in "fg" for k in range(1, X)]
    barrier = pltpu.get_barrier_semaphore()
    for to in others:
        pl.semaphore_signal(barrier, inc=1, device_id=to, device_id_type=MESH)

    home = X * f + g
    loads = [
        pltpu.make_async_copy(state_ref, S.at[c, z], in_sem.at[0]),
        pltpu.make_async_copy(goal_ref, G.at[home], in_sem.at[1]),
        pltpu.make_async_copy(pos_ref, PS.at[c], in_sem.at[2]),
    ]
    for copy in loads:
        copy.start()
    for copy in loads:
        copy.wait()
    pl.semaphore_wait(barrier, len(others))

    started = []

    def start(make, *args):
        make(*args).start()
        started.append((make, args))

    signs = (1, -1)

    def z_copy(s, k, half):
        rows = pl.ds(64 * half, 64)
        ref = S.at[c, wrap(z - s * (k - 1), Z), rows]
        i = (2 * (k - 1) + (s > 0)) * 2 + half
        return rcopy(ref, ref, ag_s.at[i], ag_r.at[i], near("z", s))

    def sib_copy(d):
        zz = wrap(z + d, Z)
        ref = S.at[c, zz]
        return rcopy(ref, ref, sb_s.at[zz], sb_r.at[zz], sibling)

    def pos_copy():
        return rcopy(PS.at[c], PS.at[c], sb_s.at[Z], sb_r.at[Z], sibling)

    def f_copy(k):
        ref = G.at[home]
        return rcopy(ref, ref, gf_s.at[k - 1], gf_r.at[k - 1], near("f", k))

    def g_copy(o, k):
        ref = G.at[X * wrap(f + o, X) + g]
        i = 3 * o + k - 1
        return rcopy(ref, ref, gg_s.at[i], gg_r.at[i], near("g", k))

    def z_piece(k, half, s):
        if k > 1:
            z_copy(s, k - 1, half).wait_recv()
        if k < H or half == (s < 0):
            start(z_copy, s, k, half)

    def z_forward(k):
        for late in (0, 1):
            for s in signs:
                z_piece(k, late ^ int(s < 0), s)
        for s in signs:
            start(sib_copy, -s * (k - 1))

    near_first = (1, 3, 2)
    for k in near_first:
        start(f_copy, k)
    for s in signs:
        z_piece(1, int(s < 0), s)
    start(pos_copy)
    MC[...] = jnp.full(MC.shape, -3e38, jnp.float32)
    SC[...] = jnp.zeros(SC.shape, jnp.float32)
    MR[...] = jnp.full(MR.shape, -3e38, jnp.float32)
    for s in signs:
        z_piece(1, int(s > 0), s)
    SR[...] = jnp.zeros(SR.shape, jnp.float32)
    for k in near_first:
        start(g_copy, 0, k)
    start(sib_copy, 0)
    z_forward(2)

    def goals_out(o):
        for k in near_first:
            start(g_copy, o, k)

    f_copy(1).wait_recv()
    goals_out(3)
    for k in (3, 2):
        f_copy(k).wait_recv()

    lanes = lax.broadcasted_iota(jnp.int32, (128, 128), 1).astype(jnp.float32)
    first_goal = (z * (2 * Q * B) + c * B).astype(jnp.float32)
    pos_copy().wait_recv()

    def spread_positive(b, carry):
        row = PS[b // Z, pl.ds(lax.rem(b, Z), 1), :].astype(jnp.float32)
        at = pl.ds(pl.multiple_of(128 * b, 128), 128)
        PB[at, :] = jnp.broadcast_to(row, (128, 128)).T - lanes - first_goal
        return carry

    lax.fori_loop(0, NB, spread_positive, 0)

    def goals_in(o):
        for k in near_first:
            g_copy(o, k).wait_recv()

    def states_in(ds):
        for d in ds:
            sib_copy(d).wait_recv()

    def unit_logits(zz, ff):
        left = S[:, pl.ds(zz, 1)].reshape(256, E)
        right = G[pl.ds(X * ff, X)].reshape(512, E)
        return lax.dot_general(left, right, (((1,), (1,)), ((), ())), preferred_element_type=jnp.float32)

    def unit_stats(zz, ff, block):
        cols = pl.ds(pl.multiple_of(512 * ff, 512), 512)
        old = MC[:, cols]
        old_top = [old[:, 128 * j : 128 * j + 128] for j in range(4)]
        col_top = list(old_top)
        rows, new_rows = [], []
        for i in range(8):
            at = pl.ds(pl.multiple_of((i // 4 * Z + zz) * 128 + 32 * (i % 4), 32), 32)
            rows.append(at)
            part = block[32 * i : 32 * i + 32] * LOG2E
            L[at, cols] = part
            p = [part[:, 128 * j : 128 * j + 128] for j in range(4)]
            best = jnp.maximum(jnp.maximum(p[0], p[1]), jnp.maximum(p[2], p[3]))
            new_rows.append(jnp.maximum(MR[at, :], best))
            for j in range(4):
                col_top[j] = jnp.maximum(col_top[j], jnp.max(p[j].reshape(4, 8, 128), axis=0))
        sums = SC[:, cols]
        col_sum = [sums[:, 128 * j : 128 * j + 128] * jnp.exp2(old_top[j] - col_top[j]) for j in range(4)]
        for i in range(8):
            part = L[rows[i], cols]
            p = [part[:, 128 * j : 128 * j + 128] for j in range(4)]
            total = SR[rows[i], :] * jnp.exp2(MR[rows[i], :] - new_rows[i])
            for j in range(4):
                total = total + jnp.exp2(p[j] - new_rows[i])
                folded = p[j].reshape(4, 8, 128)
                col_sum[j] = col_sum[j] + jnp.sum(jnp.exp2(folded - col_top[j][None]), axis=0)
            MR[rows[i], :] = new_rows[i]
            SR[rows[i], :] = total
        MC[:, cols] = jnp.concatenate(col_top, axis=1)
        SC[:, cols] = jnp.concatenate(col_sum, axis=1)

    steps = (
        ((0, 0), (1, 0), (2, 0), (3, 0)),
        ((4, 0), (5, 0), (6, 0), (0, 3)),
        ((1, 3), (2, 3), (3, 3), (4, 3)),
        ((5, 3), (6, 3), (0, 1), (1, 1)),
        ((2, 1), (3, 1), (4, 1), (5, 1)),
        ((6, 1), (0, 2), (1, 2), (2, 2)),
        ((3, 2), (4, 2), (5, 2), (6, 2)),
        ((7, 0), (7, 3), (7, 1), (7, 2)),
    )

    def arrivals(i):
        @pl.when(i == 0)
        def _():
            goals_in(0)
            z_forward(3)
            goals_out(1)
            states_in((0, 1, -1, 2))

        @pl.when(i == 1)
        def _():
            goals_out(2)
            z_forward(4)
            states_in((-2, 3, -3))
            goals_in(3)

        @pl.when(i == 3)
        def _():
            goals_in(1)

        @pl.when(i == 4)
        def _():
            for s in signs:
                z_copy(s, H, int(s < 0)).wait_recv()
            start(sib_copy, H)

        @pl.when(i == 5)
        def _():
            goals_in(2)

        @pl.when(i == 7)
        def _():
            states_in((H,))

    def step(i, carry):
        arrivals(i)
        places = []
        for j in range(4):
            n = sum(steps[m][j][0] << (3 * m) for m in range(8))
            o = sum(steps[m][j][1] << (2 * m) for m in range(8))
            n = lax.rem(jnp.right_shift(n, 3 * i), 8)
            o = lax.rem(jnp.right_shift(o, 2 * i), 4)
            away = (n + 1) // 2 * (2 * lax.rem(n, 2) - 1)
            places.append((wrap(z + away, Z), wrap(f + o, X)))
        blocks = [unit_logits(*places[0])]
        for j in range(4):
            if j < 3:
                blocks.append(unit_logits(*places[j + 1]))
            unit_stats(*places[j], blocks[j])
        return carry

    lax.fori_loop(0, 8, step, 0)

    for q in range(Q):
        m = MC[:, 128 * q : 128 * q + 128]
        top = jnp.max(m, axis=0, keepdims=True)
        total = jnp.sum(SC[:, 128 * q : 128 * q + 128] * jnp.exp2(m - top), axis=0, keepdims=True)
        LC[q : q + 1, :] = top + jnp.log2(total)

    def share_copy(axis, src, dst, me, base, k):
        return rcopy(src, dst.at[me], st_s.at[base + k], st_r.at[base + k], near(axis, k))

    def all_share(axis, n, src, dst, me, base):
        dst[me] = src[...]
        for k in range(1, n):
            start(share_copy, axis, src, dst, me, base, k)
        return [share_copy(axis, src, dst, me, base, k) for k in range(1, n)]

    def arrive(copies):
        for copy in copies:
            copy.wait_recv()

    sx = all_share("f", X, LC, xr_stat, f, 0)

    def lane_combine(b, carry):
        at = pl.ds(pl.multiple_of(128 * b, 128), 128)
        m = MR[at, :].T
        top = jnp.max(m, axis=0, keepdims=True)
        total = jnp.sum(SR[at, :].T * jnp.exp2(m - top), axis=0, keepdims=True)
        LR[pl.ds(b, 1), :] = top + jnp.log2(total)
        return carry

    lax.fori_loop(0, NB, lane_combine, 0)
    sz = all_share("z", Z, LR, zr_stat, z, 16)
    arrive(sx)
    LY[...] = combine(xr_stat[...])
    sy = all_share("g", X, LY, yr_stat, g, 8)

    def transpose_states(b, carry):
        St[:, pl.ds(pl.multiple_of(128 * b, 128), 128)] = S[b // Z, lax.rem(b, Z)].T
        return carry

    lax.fori_loop(0, NB, transpose_states, 0)

    arrive(sz)
    LS[...] = combine(zr_stat[...])
    def ls_copy():
        return rcopy(LS, sib_stat, st_s.at[0], st_r.at[0], sibling)

    start(ls_copy)
    arrive(sy)
    col_lse = combine(yr_stat[...])
    LC2 = col_lse + 1.0
    ls_copy().wait_recv()
    pair = jnp.stack([LS[...], sib_stat[...]])
    row_lse = combine(pair)
    LY2 = row_lse + 1.0
    zr_stat[0] = LY2

    xr_stat[0] = LC2
    loss_s[0] = ((row_lse + col_lse)[:8] + (row_lse + col_lse)[8:]) * (1.0 / NB)
    acc[...] = jnp.zeros(acc.shape, jnp.float32)

    def weights(ff, b, out_ref, n):
        hit_sum = acc[...]
        marks = []
        tops = []
        for j in range(X):
            q = X * ff + j
            marks.append((256 * (c * q + (1 - c) * (X * j + ff))).astype(jnp.float32))
            tops.append(xr_stat[0, pl.ds(q, 1), :])
        for i in range(8):
            at = pl.ds(pl.multiple_of(128 * b + 32 * i, 32), 32)
            rl = MR[at, :]
            pb = PB[at, :]
            for j in range(X):
                l = L[at, pl.ds(pl.multiple_of(512 * ff + 128 * j, 128), 128)]
                prob = jnp.exp2(l - rl) + jnp.exp2(l - tops[j])
                hit = pb == marks[j]
                hit_sum = hit_sum + jnp.sum(jnp.where(hit, l, 0.0).reshape(4, 8, 128), axis=0)
                out_ref[n, at, 128 * j : 128 * j + 128] = jnp.where(hit, prob - 1.0, prob).astype(jnp.bfloat16)
        acc[...] = hit_sum

    def halves(out):
        return [[out[256 * u + 64 * i : 256 * u + 64 * i + 64, :] for i in range(4)] for u in (0, 1)]

    def p1_copy(k, h):
        i = 2 * (k - 1) + h
        return rcopy(
            s1.at[k, pl.ds(2 * h, 2)], r1.at[k - 1, pl.ds(2 * h, 2)], g1_s.at[i], g1_r.at[i], near("f", k)
        )

    def goal_dot(k, h, w_ref, n, u):
        cols = pl.ds(pl.multiple_of(256 * h, 256), 256)
        out = jnp.dot(St[256 * u : 256 * u + 256, :], w_ref[n, :, cols], preferred_element_type=jnp.float32)
        for j in (0, 1):
            GG[X * wrap(f + k, X) + 2 * h + j, 256 * u : 256 * u + 256, :] = out[:, 128 * j : 128 * j + 128]
        return [
            ([out[64 * i : 64 * i + 64, 128 * j : 128 * j + 128] for i in range(4)], s1.at[k, 2 * h + j, u])
            for j in (0, 1)
        ]

    def spread_rows(b, carry):
        at = pl.ds(pl.multiple_of(128 * b, 128), 128)
        MR[at, :] = jnp.broadcast_to(zr_stat[0, pl.ds(b, 1), :], (128, 128)).T
        return carry

    lax.fori_loop(0, NB, spread_rows, 0)
    order = (2, 1, 3, 0)
    W = (W0, W1)

    def chunk_block(n, mine):
        pair = lax.rem(z // 2 + H // 2 + jnp.right_shift(156, 2 * n), H)
        return (c + (1 - mine) * (1 - 2 * c)) * Z + 2 * pair

    def state_term(b, m, out):
        rows = pl.ds(pl.multiple_of(128 * b, 256), 256)
        term = jnp.dot(
            W[m % 2][m // 2, rows, :],
            G[pl.ds(X * wrap(f + order[m], X), X)].reshape(512, E),
            preferred_element_type=jnp.float32,
        )
        return term if out is None else out + term

    def state_part(n, mine):
        b = chunk_block(n, mine)
        out = None
        for m in range(X):
            out = state_term(b, m, out)
        GS[pl.ds(b, 2)] = out.reshape(2, 128, E)

    def rb_copy(n):
        b = chunk_block(n, 0)
        pair = lax.rem(b, Z) // 2
        return rcopy(GS.at[pl.ds(b, 2)], GR.at[pl.ds(2 * pair, 2)], rb_s.at[n], rb_r.at[n], sibling)

    def rz_copy(s, u, k):
        sg = 0 if s > 0 else 1
        i = (sg * 2 + u) * H + k - 1
        return rcopy(zs.at[i], zr.at[i], rz_s.at[i], rz_r.at[i], near("z", s))

    def gs_slabs(zz, u):
        rows = pl.ds(64 * u, 64)
        return [
            GS[c * Z + zz, rows, 128 * i : 128 * i + 128] + GR[zz, rows, 128 * i : 128 * i + 128]
            for i in range(4)
        ]

    def z_step(k, lead):
        items = [(s, u) for s in signs for u in (0, 1) if lead == (u == (s < 0))]
        last = k == (H if lead else H - 1)
        ready = []
        for s, u in items:
            at = ((0 if s > 0 else 1) * 2 + u) * H + k
            slabs = gs_slabs(wrap(z + s * k, Z), u)
            if not last:
                rz_copy(s, u, k + 1).wait_recv()
                slabs = [a + b for a, b in zip(slabs, restore(zr.at[at]))]
            ready.append((slabs, zs.at[at - 1]))
        quantize_all(ready)
        for s, u in items:
            rz_copy(s, u, k).start()

    def loss_copy(stage, axis, k):
        i = 4 * stage + k if stage < 2 else 8 + k
        return rcopy(loss_s.at[stage], loss_r.at[i], st_s.at[32 + i], st_r.at[32 + i], near(axis, k))

    def loss_share(stage, axis, n):
        for k in range(1, n):
            start(loss_copy, stage, axis, k)
        return [loss_copy(stage, axis, k) for k in range(1, n)]

    def loss_add(stage, copies, slots):
        arrive(copies)
        total = loss_s[stage]
        for i in slots:
            total = total + loss_r[i]
        return total


    def part_and_give(n, carry):
        state_part(n, 0)
        rb_copy(n).start()
        return carry

    def part_only(n, carry):
        state_part(n, 1)
        return carry

    first = [chunk_block(0, mine) for mine in (0, 1)]
    for m in range(X):
        weights(wrap(f + order[m], X), first[0], W[m % 2], m // 2)
    out = None
    for m in range(X):
        out = state_term(first[0], m, out)
        weights(wrap(f + order[m], X), first[1], W[m % 2], m // 2)
    GS[pl.ds(first[0], 2)] = out.reshape(2, 128, E)
    rb_copy(0).start()
    state_part(0, 1)

    def group(n):
        def half(r, carry):
            ready = []
            for i in (1, 2, 3):
                if n > 0 and i < 3:
                    ready += goal_dot(order[n - 1], r, W[(n - 1) % 2], (n - 1) // 2, i - 1)
                weights(wrap(f + order[n], X), chunk_block(i, r), W[n % 2], n // 2)
            if n > 0:
                quantize_all(ready)
                p1_copy(order[n - 1], r).start()
            return carry

        lax.fori_loop(0, 2, half, 0)

    group(0)
    rb_copy(0).wait_recv()
    z_step(H, True)
    for n in range(1, X):
        group(n)
    loss_s[0] = loss_s[0] - 2.0 * acc[...]
    l0 = loss_share(0, "f", X)
    lax.fori_loop(1, 4, part_and_give, 0)
    lax.fori_loop(1, 4, part_only, 0)
    for n in range(1, 4):
        rb_copy(n).wait_recv()
    z_step(H - 1, False)
    z_step(H - 1, True)

    def own_goal(h, carry):
        for u in (0, 1):
            goal_dot(0, h, W[1], 1, u)
        return carry

    lax.fori_loop(0, 2, own_goal, 0)
    loss_s[1] = loss_add(0, l0, range(1, X))
    l1 = loss_share(1, "g", X)
    z_step(H - 2, False)
    z_step(H - 2, True)
    loss_s[2] = loss_add(1, l1, range(5, 4 + X))
    l2 = loss_share(2, "z", Z)

    def p2_copy(k):
        return rcopy(s2.at[k - 1], r2.at[k - 1], g2_s.at[k - 1], g2_r.at[k - 1], near("g", k))

    def summed(gg):
        blocks = halves(GG[X * f + gg])
        for k in (2, 1, 3):
            for u in (0, 1):
                blocks[u] = [a + b for a, b in zip(blocks[u], restore(r1.at[k - 1, gg, u]))]
        return blocks

    for k in (2, 1, 3):
        for h in (0, 1):
            p1_copy(k, h).wait_recv()
    for k in (2, 1, 3):
        quantize_all([(slabs, s2.at[k - 1, u]) for u, slabs in enumerate(summed(wrap(g + k, X)))])
        p2_copy(k).start()
    z_step(1, False)
    z_step(1, True)
    mine = summed(g)
    for k in (1, 3, 2):
        p2_copy(k).wait_recv()
        for u in (0, 1):
            mine[u] = [a + b for a, b in zip(mine[u], restore(r2.at[k - 1, u]))]
    for u in (0, 1):
        for i, part in enumerate(mine[u]):
            GG[home, 256 * u + 64 * i : 256 * u + 64 * i + 64, :] = part
    out_goal[...] = GG[home].T
    gg_store = pltpu.make_async_copy(out_goal, gg_out, in_sem.at[1])
    gg_store.start()
    loss_s[3] = loss_add(2, l2, range(9, 8 + Z))

    def loss_last():
        return rcopy(loss_s.at[3], loss_r.at[0], st_s.at[32], st_r.at[32], sibling)

    start(loss_last)
    for u in (0, 1):
        slabs = gs_slabs(z, u)
        for s in signs:
            rz_copy(s, u, 1).wait_recv()
            slabs = [a + b for a, b in zip(slabs, restore(zr.at[((0 if s > 0 else 1) * 2 + u) * H]))]
        for i, part in enumerate(slabs):
            GS[c * Z + z, 64 * u : 64 * u + 64, 128 * i : 128 * i + 128] = part
    gs_store = pltpu.make_async_copy(GS.at[c * Z + z], gs_out, in_sem.at[0])
    gs_store.start()
    total = loss_add(3, [loss_last()], [0])
    loss_out[0, 0] = jnp.sum(total) * (LN2 / (4.0 * Q * Z * B))

    for make, args in started:
        make(*args).wait_send()
    for n in range(4):
        rb_copy(n).wait_send()
    for k in range(1, X):
        for h in (0, 1):
            p1_copy(k, h).wait_send()
        p2_copy(k).wait_send()
    for s in signs:
        for u in (0, 1):
            for k in range(1, (H if u == (s < 0) else H - 1) + 1):
                rz_copy(s, u, k).wait_send()
    gs_store.wait()
    gg_store.wait()


def hand_over(gs_in, gg_in, loss_in, gs_out, gg_out, loss_out):
    gs_out[...] = gs_in[...]
    gg_out[...] = gg_in[...]
    loss_out[0, 0] = loss_in[0, 0]


def body(state_emb, goal_emb, positive):
    Z = lax.axis_size("gl")
    H = Z // 2
    NB = 2 * Z
    R, C = NB * B, Q * B
    vmem = pltpu.VMEM
    f32, bf16, i16 = jnp.float32, jnp.bfloat16, jnp.int16
    dma = pltpu.SemaphoreType.DMA
    scratch = [
        vmem((2, Z, B, E), bf16), vmem((Q, B, E), bf16), vmem((2, Z, B), jnp.int32),
        vmem((R, C), f32), vmem((2, R, C // 4), bf16), vmem((2, R, C // 4), bf16), vmem((E, R), bf16),
        vmem((NB, B, E), f32), vmem((Z, B, E), f32), vmem((Q, E, B), f32),
        vmem((R, B), f32), vmem((R, B), f32), vmem((R, B), f32), vmem((8, C), f32), vmem((8, C), f32),
        vmem((NB, B), f32), vmem((Z, NB, B), f32), vmem((NB, B), f32), vmem((NB, B), f32),
        vmem((Q, B), f32), vmem((X, Q, B), f32), vmem((Q, B), f32), vmem((X, Q, B), f32),
        vmem((8, B), f32),
        vmem((4 * H, UNIT, B), i16), vmem((4 * H, UNIT, B), i16),
        vmem((X, X, 2, UNIT, B), i16), vmem((X - 1, X, 2, UNIT, B), i16),
        vmem((X - 1, 2, UNIT, B), i16), vmem((X - 1, 2, UNIT, B), i16),
        vmem((4, 8, B), f32), vmem((8 + Z, 8, B), f32), vmem((B, E), f32),
        dma((3,)), dma((4 * H,)), dma((4 * H,)), dma((3,)), dma((3,)), dma((12,)), dma((12,)),
        dma((Z + 1,)), dma((Z + 1,)), dma((48,)), dma((48,)), dma((4,)), dma((4,)),
        dma((4 * H,)), dma((4 * H,)), dma((6,)), dma((6,)), dma((3,)), dma((3,)),
    ]
    there = pl.BlockSpec(memory_space=pl.ANY)
    whole = pl.BlockSpec(memory_space=pltpu.VMEM)
    scalar = pl.BlockSpec(memory_space=pltpu.SMEM)
    shapes = (
        jax.ShapeDtypeStruct((B, E), f32),
        jax.ShapeDtypeStruct((B, E), f32),
        jax.ShapeDtypeStruct((1, 1), f32),
    )
    results = pl.pallas_call(
        functools.partial(kernel, Z),
        out_shape=shapes,
        in_specs=[there] * 3,
        out_specs=(there, there, scalar),
        scratch_shapes=scratch,
        compiler_params=pltpu.CompilerParams(
            collective_id=0, has_side_effects=True, vmem_limit_bytes=62 * 1024 * 1024
        ),
    )(state_emb, goal_emb, positive.reshape(Z, B))
    grad_state, grad_goal, loss = pl.pallas_call(
        hand_over,
        out_shape=shapes,
        in_specs=[whole, whole, scalar],
        out_specs=(whole, whole, scalar),
    )(*results)
    return grad_state, grad_goal, loss.reshape(())


def solution(mesh):
    return jax.shard_map(
        body,
        mesh=mesh,
        in_specs=(P(("st", "gl"), None), P(("gl", "st"), None), P("st")),
        out_specs=(P(("st", "gl"), None), P(("gl", "st"), None), P()),
        check_vma=False,
    )
```

```python
import functools

import jax
import jax.numpy as jnp
from jax import lax
from jax.experimental import pallas as pl
from jax.experimental.pallas import tpu as pltpu
from jax.sharding import PartitionSpec as P

MESH = pl.DeviceIdType.MESH
LOG2E = 1.4426950408889634
LN2 = 0.6931471805599453
X = 4
Q = X * X
B = 128
E = 512
UNIT = 272
STEP = 32700.0


def quantize_all(items):
    tops = []
    for slabs, _ in items:
        top = jnp.abs(slabs[0])
        for slab in slabs[1:]:
            top = jnp.maximum(top, jnp.abs(slab))
        tops.append(jnp.max(top, axis=0, keepdims=True))
    powers = [jnp.ceil(jnp.log2(jnp.maximum(top, 1e-30))) for top in tops]
    factors = [jnp.exp2(-power) * STEP for power in powers]
    for (slabs, ref), power, factor in zip(items, powers, factors):
        ref[128:144, :] = jnp.broadcast_to(power, (16, 128)).astype(jnp.int32).astype(jnp.int16)
        for slab, start in zip(slabs, (0, 64, 144, 208)):
            ref[start : start + 64, :] = jnp.round(slab * factor).astype(jnp.int32).astype(jnp.int16)


def restore(ref):
    power = ref[128:144, :].astype(jnp.int32).astype(jnp.float32)[0:1, :]
    factor = jnp.exp2(power) * (1.0 / STEP)
    return [ref[s : s + 64, :].astype(jnp.int32).astype(jnp.float32) * factor for s in (0, 64, 144, 208)]


def combine(parts):
    top = jnp.max(parts, axis=0)
    return top + jnp.log2(jnp.sum(jnp.exp2(parts - top[None]), axis=0))


def kernel(
    Z, state_ref, goal_ref, pos_ref, gs_out, gg_out, loss_out,
    S, G, PS, L, W0, W1, St, GS, GR, GG, MR, SR, PB, MC, SC,
    LR, zr_stat, LS, sib_stat, LC, xr_stat, LY, yr_stat, acc,
    zs, zr, s1, r1, s2, r2, loss_s, loss_r, out_goal,
    in_sem, ag_s, ag_r, gf_s, gf_r, gg_s, gg_r, sb_s, sb_r, st_s, st_r, rb_s, rb_r, rz_s, rz_r,
    g1_s, g1_r, g2_s, g2_r,
):
    st = lax.axis_index("st")
    z = lax.axis_index("gl")
    c = lax.rem(st, 2)
    chip = st // 2
    x = lax.rem(chip, X)
    y = chip // X
    H = Z // 2
    NB = 2 * Z

    def wrap(v, n):
        return lax.rem(v + n, n)

    def dev(xx, yy, zz, cc):
        return ((yy * X + xx) * 2 + cc, zz)

    sibling = dev(x, y, z, 1 - c)

    f = x + c * (y - x)
    g = y + c * (x - y)

    def near(axis, k):
        if axis == "z":
            return dev(x, y, wrap(z + k, Z), c)
        ff, gg = (wrap(f + k, X), g) if axis == "f" else (f, wrap(g + k, X))
        return dev(ff + c * (gg - ff), gg + c * (ff - gg), z, c)

    def rcopy(src, dst, send, recv, to):
        return pltpu.make_async_remote_copy(
            src_ref=src, dst_ref=dst, send_sem=send, recv_sem=recv, device_id=to, device_id_type=MESH
        )

    others = [sibling]
    others += [near("z", k) for k in range(1, Z)]
    others += [near(a, k) for a in "fg" for k in range(1, X)]
    barrier = pltpu.get_barrier_semaphore()
    for to in others:
        pl.semaphore_signal(barrier, inc=1, device_id=to, device_id_type=MESH)

    home = X * f + g
    loads = [
        pltpu.make_async_copy(state_ref, S.at[c, z], in_sem.at[0]),
        pltpu.make_async_copy(goal_ref, G.at[home], in_sem.at[1]),
        pltpu.make_async_copy(pos_ref, PS.at[c], in_sem.at[2]),
    ]
    for copy in loads:
        copy.start()
    for copy in loads:
        copy.wait()
    pl.semaphore_wait(barrier, len(others))

    started = []

    def start(make, *args):
        make(*args).start()
        started.append((make, args))

    signs = (1, -1)

    def z_copy(s, k, half):
        rows = pl.ds(64 * half, 64)
        ref = S.at[c, wrap(z - s * (k - 1), Z), rows]
        i = (2 * (k - 1) + (s > 0)) * 2 + half
        return rcopy(ref, ref, ag_s.at[i], ag_r.at[i], near("z", s))

    def sib_copy(d):
        zz = wrap(z + d, Z)
        ref = S.at[c, zz]
        return rcopy(ref, ref, sb_s.at[zz], sb_r.at[zz], sibling)

    def pos_copy():
        return rcopy(PS.at[c], PS.at[c], sb_s.at[Z], sb_r.at[Z], sibling)

    def f_copy(k):
        ref = G.at[home]
        return rcopy(ref, ref, gf_s.at[k - 1], gf_r.at[k - 1], near("f", k))

    def g_copy(o, k):
        ref = G.at[X * wrap(f + o, X) + g]
        i = 3 * o + k - 1
        return rcopy(ref, ref, gg_s.at[i], gg_r.at[i], near("g", k))

    def z_piece(k, half, s):
        if k > 1:
            z_copy(s, k - 1, half).wait_recv()
        if k < H or half == (s < 0):
            start(z_copy, s, k, half)

    def z_forward(k):
        for late in (0, 1):
            for s in signs:
                z_piece(k, late ^ int(s < 0), s)
        for s in signs:
            start(sib_copy, -s * (k - 1))

    near_first = (1, 3, 2)
    for k in near_first:
        start(f_copy, k)
    for s in signs:
        z_piece(1, int(s < 0), s)
    start(pos_copy)
    MC[...] = jnp.full(MC.shape, -3e38, jnp.float32)
    SC[...] = jnp.zeros(SC.shape, jnp.float32)
    MR[...] = jnp.full(MR.shape, -3e38, jnp.float32)
    for s in signs:
        z_piece(1, int(s > 0), s)
    SR[...] = jnp.zeros(SR.shape, jnp.float32)
    for k in near_first:
        start(g_copy, 0, k)
    start(sib_copy, 0)
    z_forward(2)

    def goals_out(o):
        for k in near_first:
            start(g_copy, o, k)

    f_copy(1).wait_recv()
    goals_out(3)
    for k in (3, 2):
        f_copy(k).wait_recv()

    lanes = lax.broadcasted_iota(jnp.int32, (128, 128), 1).astype(jnp.float32)
    first_goal = (z * (2 * Q * B) + c * B).astype(jnp.float32)
    pos_copy().wait_recv()

    def spread_positive(b, carry):
        row = PS[b // Z, pl.ds(lax.rem(b, Z), 1), :].astype(jnp.float32)
        at = pl.ds(pl.multiple_of(128 * b, 128), 128)
        PB[at, :] = jnp.broadcast_to(row, (128, 128)).T - lanes - first_goal
        return carry

    lax.fori_loop(0, NB, spread_positive, 0)

    def goals_in(o):
        for k in near_first:
            g_copy(o, k).wait_recv()

    def states_in(ds):
        for d in ds:
            sib_copy(d).wait_recv()

    def unit_logits(zz, ff):
        left = S[:, pl.ds(zz, 1)].reshape(256, E)
        right = G[pl.ds(X * ff, X)].reshape(512, E)
        return lax.dot_general(left, right, (((1,), (1,)), ((), ())), preferred_element_type=jnp.float32)

    def unit_stats(zz, ff, block):
        cols = pl.ds(pl.multiple_of(512 * ff, 512), 512)
        old = MC[:, cols]
        old_top = [old[:, 128 * j : 128 * j + 128] for j in range(4)]
        col_top = list(old_top)
        rows, new_rows = [], []
        for i in range(8):
            at = pl.ds(pl.multiple_of((i // 4 * Z + zz) * 128 + 32 * (i % 4), 32), 32)
            rows.append(at)
            part = block[32 * i : 32 * i + 32] * LOG2E
            L[at, cols] = part
            p = [part[:, 128 * j : 128 * j + 128] for j in range(4)]
            best = jnp.maximum(jnp.maximum(p[0], p[1]), jnp.maximum(p[2], p[3]))
            new_rows.append(jnp.maximum(MR[at, :], best))
            for j in range(4):
                col_top[j] = jnp.maximum(col_top[j], jnp.max(p[j].reshape(4, 8, 128), axis=0))
        sums = SC[:, cols]
        col_sum = [sums[:, 128 * j : 128 * j + 128] * jnp.exp2(old_top[j] - col_top[j]) for j in range(4)]
        for i in range(8):
            part = L[rows[i], cols]
            p = [part[:, 128 * j : 128 * j + 128] for j in range(4)]
            total = SR[rows[i], :] * jnp.exp2(MR[rows[i], :] - new_rows[i])
            for j in range(4):
                total = total + jnp.exp2(p[j] - new_rows[i])
                folded = p[j].reshape(4, 8, 128)
                col_sum[j] = col_sum[j] + jnp.sum(jnp.exp2(folded - col_top[j][None]), axis=0)
            MR[rows[i], :] = new_rows[i]
            SR[rows[i], :] = total
        MC[:, cols] = jnp.concatenate(col_top, axis=1)
        SC[:, cols] = jnp.concatenate(col_sum, axis=1)

    steps = (
        ((0, 0), (1, 0), (2, 0), (3, 0)),
        ((4, 0), (5, 0), (6, 0), (0, 3)),
        ((1, 3), (2, 3), (3, 3), (4, 3)),
        ((5, 3), (6, 3), (0, 1), (1, 1)),
        ((2, 1), (3, 1), (4, 1), (5, 1)),
        ((6, 1), (0, 2), (1, 2), (2, 2)),
        ((3, 2), (4, 2), (5, 2), (6, 2)),
        ((7, 0), (7, 3), (7, 1), (7, 2)),
    )

    def arrivals(i):
        @pl.when(i == 0)
        def _():
            goals_in(0)
            z_forward(3)
            goals_out(1)
            states_in((0, 1, -1, 2))

        @pl.when(i == 1)
        def _():
            goals_out(2)
            z_forward(4)
            states_in((-2, 3, -3))
            goals_in(3)

        @pl.when(i == 3)
        def _():
            goals_in(1)

        @pl.when(i == 4)
        def _():
            for s in signs:
                z_copy(s, H, int(s < 0)).wait_recv()
            start(sib_copy, H)

        @pl.when(i == 5)
        def _():
            goals_in(2)

        @pl.when(i == 7)
        def _():
            states_in((H,))

    def step(i, carry):
        arrivals(i)
        places = []
        for j in range(4):
            n = sum(steps[m][j][0] << (3 * m) for m in range(8))
            o = sum(steps[m][j][1] << (2 * m) for m in range(8))
            n = lax.rem(jnp.right_shift(n, 3 * i), 8)
            o = lax.rem(jnp.right_shift(o, 2 * i), 4)
            away = (n + 1) // 2 * (2 * lax.rem(n, 2) - 1)
            places.append((wrap(z + away, Z), wrap(f + o, X)))
        blocks = [unit_logits(*places[0])]
        for j in range(4):
            if j < 3:
                blocks.append(unit_logits(*places[j + 1]))
            unit_stats(*places[j], blocks[j])
        return carry

    lax.fori_loop(0, 8, step, 0)

    for q in range(Q):
        m = MC[:, 128 * q : 128 * q + 128]
        top = jnp.max(m, axis=0, keepdims=True)
        total = jnp.sum(SC[:, 128 * q : 128 * q + 128] * jnp.exp2(m - top), axis=0, keepdims=True)
        LC[q : q + 1, :] = top + jnp.log2(total)

    def share_copy(axis, src, dst, me, base, k):
        return rcopy(src, dst.at[me], st_s.at[base + k], st_r.at[base + k], near(axis, k))

    def all_share(axis, n, src, dst, me, base):
        dst[me] = src[...]
        for k in range(1, n):
            start(share_copy, axis, src, dst, me, base, k)
        return [share_copy(axis, src, dst, me, base, k) for k in range(1, n)]

    def arrive(copies):
        for copy in copies:
            copy.wait_recv()

    sx = all_share("f", X, LC, xr_stat, f, 0)

    def lane_combine(b, carry):
        at = pl.ds(pl.multiple_of(128 * b, 128), 128)
        m = MR[at, :].T
        top = jnp.max(m, axis=0, keepdims=True)
        total = jnp.sum(SR[at, :].T * jnp.exp2(m - top), axis=0, keepdims=True)
        LR[pl.ds(b, 1), :] = top + jnp.log2(total)
        return carry

    lax.fori_loop(0, NB, lane_combine, 0)
    sz = all_share("z", Z, LR, zr_stat, z, 16)
    arrive(sx)
    LY[...] = combine(xr_stat[...])
    sy = all_share("g", X, LY, yr_stat, g, 8)

    def transpose_states(b, carry):
        St[:, pl.ds(pl.multiple_of(128 * b, 128), 128)] = S[b // Z, lax.rem(b, Z)].T
        return carry

    lax.fori_loop(0, NB, transpose_states, 0)

    arrive(sz)
    LS[...] = combine(zr_stat[...])
    def ls_copy():
        return rcopy(LS, sib_stat, st_s.at[0], st_r.at[0], sibling)

    start(ls_copy)
    arrive(sy)
    col_lse = combine(yr_stat[...])
    LC2 = col_lse + 1.0
    ls_copy().wait_recv()
    pair = jnp.stack([LS[...], sib_stat[...]])
    row_lse = combine(pair)
    LY2 = row_lse + 1.0
    zr_stat[0] = LY2

    xr_stat[0] = LC2
    loss_s[0] = ((row_lse + col_lse)[:8] + (row_lse + col_lse)[8:]) * (1.0 / NB)
    acc[...] = jnp.zeros(acc.shape, jnp.float32)

    def weights(ff, b, out_ref, n):
        hit_sum = acc[...]
        marks = []
        tops = []
        for j in range(X):
            q = X * ff + j
            marks.append((256 * (c * q + (1 - c) * (X * j + ff))).astype(jnp.float32))
            tops.append(xr_stat[0, pl.ds(q, 1), :])
        for i in range(8):
            at = pl.ds(pl.multiple_of(128 * b + 32 * i, 32), 32)
            rl = MR[at, :]
            pb = PB[at, :]
            for j in range(X):
                l = L[at, pl.ds(pl.multiple_of(512 * ff + 128 * j, 128), 128)]
                prob = jnp.exp2(l - rl) + jnp.exp2(l - tops[j])
                hit = pb == marks[j]
                hit_sum = hit_sum + jnp.sum(jnp.where(hit, l, 0.0).reshape(4, 8, 128), axis=0)
                out_ref[n, at, 128 * j : 128 * j + 128] = jnp.where(hit, prob - 1.0, prob).astype(jnp.bfloat16)
        acc[...] = hit_sum

    def halves(out):
        return [[out[256 * u + 64 * i : 256 * u + 64 * i + 64, :] for i in range(4)] for u in (0, 1)]

    def p1_copy(k, h):
        i = 2 * (k - 1) + h
        return rcopy(
            s1.at[k, pl.ds(2 * h, 2)], r1.at[k - 1, pl.ds(2 * h, 2)], g1_s.at[i], g1_r.at[i], near("f", k)
        )

    def goal_dot(k, h, w_ref, n, u):
        cols = pl.ds(pl.multiple_of(256 * h, 256), 256)
        out = jnp.dot(St[256 * u : 256 * u + 256, :], w_ref[n, :, cols], preferred_element_type=jnp.float32)
        for j in (0, 1):
            GG[X * wrap(f + k, X) + 2 * h + j, 256 * u : 256 * u + 256, :] = out[:, 128 * j : 128 * j + 128]
        return [
            ([out[64 * i : 64 * i + 64, 128 * j : 128 * j + 128] for i in range(4)], s1.at[k, 2 * h + j, u])
            for j in (0, 1)
        ]

    def spread_rows(b, carry):
        at = pl.ds(pl.multiple_of(128 * b, 128), 128)
        MR[at, :] = jnp.broadcast_to(zr_stat[0, pl.ds(b, 1), :], (128, 128)).T
        return carry

    lax.fori_loop(0, NB, spread_rows, 0)
    order = (2, 1, 3, 0)
    W = (W0, W1)

    def chunk_block(n, mine):
        pair = lax.rem(z // 2 + H // 2 + jnp.right_shift(156, 2 * n), H)
        return (c + (1 - mine) * (1 - 2 * c)) * Z + 2 * pair

    def state_term(b, m, out):
        rows = pl.ds(pl.multiple_of(128 * b, 256), 256)
        term = jnp.dot(
            W[m % 2][m // 2, rows, :],
            G[pl.ds(X * wrap(f + order[m], X), X)].reshape(512, E),
            preferred_element_type=jnp.float32,
        )
        return term if out is None else out + term

    def state_part(n, mine):
        b = chunk_block(n, mine)
        out = None
        for m in range(X):
            out = state_term(b, m, out)
        GS[pl.ds(b, 2)] = out.reshape(2, 128, E)

    def rb_copy(n):
        b = chunk_block(n, 0)
        pair = lax.rem(b, Z) // 2
        return rcopy(GS.at[pl.ds(b, 2)], GR.at[pl.ds(2 * pair, 2)], rb_s.at[n], rb_r.at[n], sibling)

    def rz_copy(s, u, k):
        sg = 0 if s > 0 else 1
        i = (sg * 2 + u) * H + k - 1
        return rcopy(zs.at[i], zr.at[i], rz_s.at[i], rz_r.at[i], near("z", s))

    def gs_slabs(zz, u):
        rows = pl.ds(64 * u, 64)
        return [
            GS[c * Z + zz, rows, 128 * i : 128 * i + 128] + GR[zz, rows, 128 * i : 128 * i + 128]
            for i in range(4)
        ]

    def z_step(k, lead):
        items = [(s, u) for s in signs for u in (0, 1) if lead == (u == (s < 0))]
        last = k == (H if lead else H - 1)
        ready = []
        for s, u in items:
            at = ((0 if s > 0 else 1) * 2 + u) * H + k
            slabs = gs_slabs(wrap(z + s * k, Z), u)
            if not last:
                rz_copy(s, u, k + 1).wait_recv()
                slabs = [a + b for a, b in zip(slabs, restore(zr.at[at]))]
            ready.append((slabs, zs.at[at - 1]))
        quantize_all(ready)
        for s, u in items:
            rz_copy(s, u, k).start()

    def loss_copy(stage, k):
        i = (0, 0, 4, 8)[stage] + k
        to = sibling if stage == 0 else near(" fgz"[stage], k)
        return rcopy(loss_s.at[stage], loss_r.at[i], st_s.at[32 + i], st_r.at[32 + i], to)

    loss_peers = ((0,), range(1, X), range(1, X), range(1, Z))

    def loss_share(stage):
        for k in loss_peers[stage]:
            start(loss_copy, stage, k)

    def loss_add(stage):
        total = loss_s[stage]
        for k in loss_peers[stage]:
            loss_copy(stage, k).wait_recv()
            total = total + loss_r[(0, 0, 4, 8)[stage] + k]
        return total

    def part_and_give(n, carry):
        state_part(n, 0)
        rb_copy(n).start()
        return carry

    def part_only(n, carry):
        state_part(n, 1)
        return carry

    first = [chunk_block(0, mine) for mine in (0, 1)]
    for m in range(X):
        weights(wrap(f + order[m], X), first[0], W[m % 2], m // 2)
    out = None
    for m in range(X):
        out = state_term(first[0], m, out)
        weights(wrap(f + order[m], X), first[1], W[m % 2], m // 2)
    GS[pl.ds(first[0], 2)] = out.reshape(2, 128, E)
    rb_copy(0).start()
    state_part(0, 1)

    def group(n):
        def half(r, carry):
            for i in (1, 2, 3):
                weights(wrap(f + order[n], X), chunk_block(i, r), W[n % 2], n // 2)
            return carry

        lax.fori_loop(0, 2, half, 0)

    def goals(n):
        def half(h, carry):
            ready = goal_dot(order[n], h, W[n % 2], n // 2, 0)
            ready += goal_dot(order[n], h, W[n % 2], n // 2, 1)
            if order[n] > 0:
                quantize_all(ready)
                p1_copy(order[n], h).start()
            return carry

        lax.fori_loop(0, 2, half, 0)

    for n in range(X):
        group(n)
        if n < X - 1:
            goals(n)
        if n == 0:
            rb_copy(0).wait_recv()
            z_step(H, True)
    loss_s[0] = loss_s[0] - 2.0 * acc[...]
    loss_share(0)
    lax.fori_loop(1, 3, part_and_give, 0)
    loss_s[1] = loss_add(0)
    loss_share(1)
    lax.fori_loop(1, 3, part_only, 0)
    for n in (1, 2):
        rb_copy(n).wait_recv()
    z_step(H - 1, True)
    z_step(H - 1, False)
    lax.fori_loop(3, 4, part_and_give, 0)
    lax.fori_loop(3, 4, part_only, 0)
    goals(X - 1)
    rb_copy(3).wait_recv()
    loss_s[2] = loss_add(1)
    loss_share(2)
    z_step(H - 2, True)
    z_step(H - 2, False)

    def p2_copy(k):
        return rcopy(s2.at[k - 1], r2.at[k - 1], g2_s.at[k - 1], g2_r.at[k - 1], near("g", k))

    def summed(gg):
        blocks = halves(GG[X * f + gg])
        for k in (2, 1, 3):
            for u in (0, 1):
                blocks[u] = [a + b for a, b in zip(blocks[u], restore(r1.at[k - 1, gg, u]))]
        return blocks

    for k in (2, 1, 3):
        for h in (0, 1):
            p1_copy(k, h).wait_recv()
    for k in (2, 1, 3):
        quantize_all([(slabs, s2.at[k - 1, u]) for u, slabs in enumerate(summed(wrap(g + k, X)))])
        p2_copy(k).start()
    loss_s[3] = loss_add(2)
    loss_share(3)
    z_step(1, True)
    z_step(1, False)
    mine = summed(g)
    for k in (1, 3, 2):
        p2_copy(k).wait_recv()
        for u in (0, 1):
            mine[u] = [a + b for a, b in zip(mine[u], restore(r2.at[k - 1, u]))]
    for u in (0, 1):
        for i, part in enumerate(mine[u]):
            GG[home, 256 * u + 64 * i : 256 * u + 64 * i + 64, :] = part
    out_goal[...] = GG[home].T
    gg_store = pltpu.make_async_copy(out_goal, gg_out, in_sem.at[1])
    gg_store.start()
    for u in (0, 1):
        slabs = gs_slabs(z, u)
        for s in signs:
            rz_copy(s, u, 1).wait_recv()
            slabs = [a + b for a, b in zip(slabs, restore(zr.at[((0 if s > 0 else 1) * 2 + u) * H]))]
        for i, part in enumerate(slabs):
            GS[c * Z + z, 64 * u : 64 * u + 64, 128 * i : 128 * i + 128] = part
    gs_store = pltpu.make_async_copy(GS.at[c * Z + z], gs_out, in_sem.at[0])
    gs_store.start()
    total = loss_add(3)
    loss_out[0, 0] = jnp.sum(total) * (LN2 / (4.0 * Q * Z * B))

    for make, args in started:
        make(*args).wait_send()
    for n in range(4):
        rb_copy(n).wait_send()
    for k in range(1, X):
        for h in (0, 1):
            p1_copy(k, h).wait_send()
        p2_copy(k).wait_send()
    for s in signs:
        for u in (0, 1):
            for k in range(1, (H if u == (s < 0) else H - 1) + 1):
                rz_copy(s, u, k).wait_send()
    gs_store.wait()
    gg_store.wait()


def hand_over(gs_in, gg_in, loss_in, gs_out, gg_out, loss_out):
    gs_out[...] = gs_in[...]
    gg_out[...] = gg_in[...]
    loss_out[0, 0] = loss_in[0, 0]


def body(state_emb, goal_emb, positive):
    Z = lax.axis_size("gl")
    H = Z // 2
    NB = 2 * Z
    R, C = NB * B, Q * B
    vmem = pltpu.VMEM
    f32, bf16, i16 = jnp.float32, jnp.bfloat16, jnp.int16
    dma = pltpu.SemaphoreType.DMA
    scratch = [
        vmem((2, Z, B, E), bf16), vmem((Q, B, E), bf16), vmem((2, Z, B), jnp.int32),
        vmem((R, C), f32), vmem((2, R, C // 4), bf16), vmem((2, R, C // 4), bf16), vmem((E, R), bf16),
        vmem((NB, B, E), f32), vmem((Z, B, E), f32), vmem((Q, E, B), f32),
        vmem((R, B), f32), vmem((R, B), f32), vmem((R, B), f32), vmem((8, C), f32), vmem((8, C), f32),
        vmem((NB, B), f32), vmem((Z, NB, B), f32), vmem((NB, B), f32), vmem((NB, B), f32),
        vmem((Q, B), f32), vmem((X, Q, B), f32), vmem((Q, B), f32), vmem((X, Q, B), f32),
        vmem((8, B), f32),
        vmem((4 * H, UNIT, B), i16), vmem((4 * H, UNIT, B), i16),
        vmem((X, X, 2, UNIT, B), i16), vmem((X - 1, X, 2, UNIT, B), i16),
        vmem((X - 1, 2, UNIT, B), i16), vmem((X - 1, 2, UNIT, B), i16),
        vmem((4, 8, B), f32), vmem((8 + Z, 8, B), f32), vmem((B, E), f32),
        dma((3,)), dma((4 * H,)), dma((4 * H,)), dma((3,)), dma((3,)), dma((12,)), dma((12,)),
        dma((Z + 1,)), dma((Z + 1,)), dma((48,)), dma((48,)), dma((4,)), dma((4,)),
        dma((4 * H,)), dma((4 * H,)), dma((6,)), dma((6,)), dma((3,)), dma((3,)),
    ]
    there = pl.BlockSpec(memory_space=pl.ANY)
    whole = pl.BlockSpec(memory_space=pltpu.VMEM)
    scalar = pl.BlockSpec(memory_space=pltpu.SMEM)
    shapes = (
        jax.ShapeDtypeStruct((B, E), f32),
        jax.ShapeDtypeStruct((B, E), f32),
        jax.ShapeDtypeStruct((1, 1), f32),
    )
    results = pl.pallas_call(
        functools.partial(kernel, Z),
        out_shape=shapes,
        in_specs=[there] * 3,
        out_specs=(there, there, scalar),
        scratch_shapes=scratch,
        compiler_params=pltpu.CompilerParams(
            collective_id=0, has_side_effects=True, vmem_limit_bytes=62 * 1024 * 1024
        ),
    )(state_emb, goal_emb, positive.reshape(Z, B))
    grad_state, grad_goal, loss = pl.pallas_call(
        hand_over,
        out_shape=shapes,
        in_specs=[whole, whole, scalar],
        out_specs=(whole, whole, scalar),
    )(*results)
    return grad_state, grad_goal, loss.reshape(())


def solution(mesh):
    return jax.shard_map(
        body,
        mesh=mesh,
        in_specs=(P(("st", "gl"), None), P(("gl", "st"), None), P("st")),
        out_specs=(P(("st", "gl"), None), P(("gl", "st"), None), P()),
        check_vma=False,
    )
```

```python
import functools

import jax
import jax.numpy as jnp
from jax import lax
from jax.experimental import pallas as pl
from jax.experimental.pallas import tpu as pltpu
from jax.sharding import PartitionSpec as P

MESH = pl.DeviceIdType.MESH
LOG2E = 1.4426950408889634
LN2 = 0.6931471805599453
X = 4
Q = X * X
B = 128
E = 512
UNIT = 272
STEP = 32700.0


def quantize_all(items):
    tops = []
    for slabs, _ in items:
        top = jnp.abs(slabs[0])
        for slab in slabs[1:]:
            top = jnp.maximum(top, jnp.abs(slab))
        tops.append(jnp.max(top, axis=0, keepdims=True))
    powers = [jnp.ceil(jnp.log2(jnp.maximum(top, 1e-30))) for top in tops]
    factors = [jnp.exp2(-power) * STEP for power in powers]
    for (slabs, ref), power, factor in zip(items, powers, factors):
        ref[128:144, :] = jnp.broadcast_to(power, (16, 128)).astype(jnp.int32).astype(jnp.int16)
        for slab, start in zip(slabs, (0, 64, 144, 208)):
            ref[start : start + 64, :] = jnp.round(slab * factor).astype(jnp.int32).astype(jnp.int16)


def restore(ref):
    power = ref[128:144, :].astype(jnp.int32).astype(jnp.float32)[0:1, :]
    factor = jnp.exp2(power) * (1.0 / STEP)
    return [ref[s : s + 64, :].astype(jnp.int32).astype(jnp.float32) * factor for s in (0, 64, 144, 208)]


def combine(parts):
    top = jnp.max(parts, axis=0)
    return top + jnp.log2(jnp.sum(jnp.exp2(parts - top[None]), axis=0))


def kernel(
    Z, state_ref, goal_ref, pos_ref, gs_out, gg_out, loss_out,
    S, G, PS, L, W0, W1, St, GS, GR, GG, MR, SR, PB, MC, SC,
    LR, zr_stat, LS, sib_stat, LC, xr_stat, LY, yr_stat, acc,
    zs, zr, s1, r1, s2, r2, loss_s, loss_r, out_goal,
    in_sem, ag_s, ag_r, gf_s, gf_r, gg_s, gg_r, sb_s, sb_r, st_s, st_r, rb_s, rb_r, rz_s, rz_r,
    g1_s, g1_r, g2_s, g2_r,
):
    st = lax.axis_index("st")
    z = lax.axis_index("gl")
    c = lax.rem(st, 2)
    chip = st // 2
    x = lax.rem(chip, X)
    y = chip // X
    H = Z // 2
    NB = 2 * Z

    def wrap(v, n):
        return lax.rem(v + n, n)

    def dev(xx, yy, zz, cc):
        return ((yy * X + xx) * 2 + cc, zz)

    sibling = dev(x, y, z, 1 - c)

    f = x + c * (y - x)
    g = y + c * (x - y)

    def near(axis, k):
        if axis == "z":
            return dev(x, y, wrap(z + k, Z), c)
        ff, gg = (wrap(f + k, X), g) if axis == "f" else (f, wrap(g + k, X))
        return dev(ff + c * (gg - ff), gg + c * (ff - gg), z, c)

    def rcopy(src, dst, send, recv, to):
        return pltpu.make_async_remote_copy(
            src_ref=src, dst_ref=dst, send_sem=send, recv_sem=recv, device_id=to, device_id_type=MESH
        )

    others = [sibling]
    others += [near("z", k) for k in range(1, Z)]
    others += [near(a, k) for a in "fg" for k in range(1, X)]
    barrier = pltpu.get_barrier_semaphore()
    for to in others:
        pl.semaphore_signal(barrier, inc=1, device_id=to, device_id_type=MESH)

    home = X * f + g
    loads = [
        pltpu.make_async_copy(state_ref, S.at[c, z], in_sem.at[0]),
        pltpu.make_async_copy(goal_ref, G.at[home], in_sem.at[1]),
        pltpu.make_async_copy(pos_ref, PS.at[c], in_sem.at[2]),
    ]
    for copy in loads:
        copy.start()
    for copy in loads:
        copy.wait()
    pl.semaphore_wait(barrier, len(others))

    started = []

    def start(make, *args):
        make(*args).start()
        started.append((make, args))

    signs = (1, -1)

    def z_copy(s, k, half):
        rows = pl.ds(64 * half, 64)
        ref = S.at[c, wrap(z - s * (k - 1), Z), rows]
        i = (2 * (k - 1) + (s > 0)) * 2 + half
        return rcopy(ref, ref, ag_s.at[i], ag_r.at[i], near("z", s))

    def sib_copy(d):
        zz = wrap(z + d, Z)
        ref = S.at[c, zz]
        return rcopy(ref, ref, sb_s.at[zz], sb_r.at[zz], sibling)

    def pos_copy():
        return rcopy(PS.at[c], PS.at[c], sb_s.at[Z], sb_r.at[Z], sibling)

    def f_copy(k):
        ref = G.at[home]
        return rcopy(ref, ref, gf_s.at[k - 1], gf_r.at[k - 1], near("f", k))

    def g_copy(o, k):
        ref = G.at[X * wrap(f + o, X) + g]
        i = 3 * o + k - 1
        return rcopy(ref, ref, gg_s.at[i], gg_r.at[i], near("g", k))

    def z_piece(k, half, s):
        if k > 1:
            z_copy(s, k - 1, half).wait_recv()
        if k < H or half == (s < 0):
            start(z_copy, s, k, half)

    def z_forward(k):
        for late in (0, 1):
            for s in signs:
                z_piece(k, late ^ int(s < 0), s)
        for s in signs:
            start(sib_copy, -s * (k - 1))

    near_first = (1, 3, 2)
    for k in near_first:
        start(f_copy, k)
    for s in signs:
        z_piece(1, int(s < 0), s)
    start(pos_copy)
    MC[...] = jnp.full(MC.shape, -3e38, jnp.float32)
    SC[...] = jnp.zeros(SC.shape, jnp.float32)
    MR[...] = jnp.full(MR.shape, -3e38, jnp.float32)
    for s in signs:
        z_piece(1, int(s > 0), s)
    SR[...] = jnp.zeros(SR.shape, jnp.float32)
    for k in near_first:
        start(g_copy, 0, k)
    start(sib_copy, 0)
    z_forward(2)

    def goals_out(o):
        for k in near_first:
            start(g_copy, o, k)

    f_copy(1).wait_recv()
    goals_out(3)
    for k in (3, 2):
        f_copy(k).wait_recv()

    lanes = lax.broadcasted_iota(jnp.int32, (128, 128), 1).astype(jnp.float32)
    first_goal = (z * (2 * Q * B) + c * B).astype(jnp.float32)
    pos_copy().wait_recv()

    def spread_positive(b, carry):
        row = PS[b // Z, pl.ds(lax.rem(b, Z), 1), :].astype(jnp.float32)
        at = pl.ds(pl.multiple_of(128 * b, 128), 128)
        PB[at, :] = jnp.broadcast_to(row, (128, 128)).T - lanes - first_goal
        return carry

    lax.fori_loop(0, NB, spread_positive, 0)

    def goals_in(o):
        for k in near_first:
            g_copy(o, k).wait_recv()

    def states_in(ds):
        for d in ds:
            sib_copy(d).wait_recv()

    def unit_logits(zz, ff):
        left = S[:, pl.ds(zz, 1)].reshape(256, E)
        right = G[pl.ds(X * ff, X)].reshape(512, E)
        return lax.dot_general(left, right, (((1,), (1,)), ((), ())), preferred_element_type=jnp.float32)

    def unit_stats(zz, ff, block):
        cols = pl.ds(pl.multiple_of(512 * ff, 512), 512)
        old = MC[:, cols]
        old_top = [old[:, 128 * j : 128 * j + 128] for j in range(4)]
        col_top = list(old_top)
        rows, new_rows = [], []
        for i in range(8):
            at = pl.ds(pl.multiple_of((i // 4 * Z + zz) * 128 + 32 * (i % 4), 32), 32)
            rows.append(at)
            part = block[32 * i : 32 * i + 32] * LOG2E
            L[at, cols] = part
            p = [part[:, 128 * j : 128 * j + 128] for j in range(4)]
            best = jnp.maximum(jnp.maximum(p[0], p[1]), jnp.maximum(p[2], p[3]))
            new_rows.append(jnp.maximum(MR[at, :], best))
            for j in range(4):
                col_top[j] = jnp.maximum(col_top[j], jnp.max(p[j].reshape(4, 8, 128), axis=0))
        sums = SC[:, cols]
        col_sum = [sums[:, 128 * j : 128 * j + 128] * jnp.exp2(old_top[j] - col_top[j]) for j in range(4)]
        for i in range(8):
            part = L[rows[i], cols]
            p = [part[:, 128 * j : 128 * j + 128] for j in range(4)]
            total = SR[rows[i], :] * jnp.exp2(MR[rows[i], :] - new_rows[i])
            for j in range(4):
                total = total + jnp.exp2(p[j] - new_rows[i])
                folded = p[j].reshape(4, 8, 128)
                col_sum[j] = col_sum[j] + jnp.sum(jnp.exp2(folded - col_top[j][None]), axis=0)
            MR[rows[i], :] = new_rows[i]
            SR[rows[i], :] = total
        MC[:, cols] = jnp.concatenate(col_top, axis=1)
        SC[:, cols] = jnp.concatenate(col_sum, axis=1)

    steps = (
        ((0, 0), (1, 0), (2, 0), (3, 0)),
        ((4, 0), (5, 0), (6, 0), (0, 3)),
        ((1, 3), (2, 3), (3, 3), (4, 3)),
        ((5, 3), (6, 3), (0, 1), (1, 1)),
        ((2, 1), (3, 1), (4, 1), (5, 1)),
        ((6, 1), (0, 2), (1, 2), (2, 2)),
        ((3, 2), (4, 2), (5, 2), (6, 2)),
        ((7, 0), (7, 3), (7, 1), (7, 2)),
    )

    def arrivals(i):
        @pl.when(i == 0)
        def _():
            goals_in(0)
            z_forward(3)
            goals_out(1)
            states_in((0, 1, -1, 2))

        @pl.when(i == 1)
        def _():
            goals_out(2)
            z_forward(4)
            states_in((-2, 3, -3))
            goals_in(3)

        @pl.when(i == 3)
        def _():
            goals_in(1)

        @pl.when(i == 4)
        def _():
            for s in signs:
                z_copy(s, H, int(s < 0)).wait_recv()
            start(sib_copy, H)

        @pl.when(i == 5)
        def _():
            goals_in(2)

        @pl.when(i == 7)
        def _():
            states_in((H,))

    def step(i, carry):
        arrivals(i)
        places = []
        for j in range(4):
            n = sum(steps[m][j][0] << (3 * m) for m in range(8))
            o = sum(steps[m][j][1] << (2 * m) for m in range(8))
            n = lax.rem(jnp.right_shift(n, 3 * i), 8)
            o = lax.rem(jnp.right_shift(o, 2 * i), 4)
            away = (n + 1) // 2 * (2 * lax.rem(n, 2) - 1)
            places.append((wrap(z + away, Z), wrap(f + o, X)))
        blocks = [unit_logits(*places[0])]
        for j in range(4):
            if j < 3:
                blocks.append(unit_logits(*places[j + 1]))
            unit_stats(*places[j], blocks[j])
        return carry

    lax.fori_loop(0, 8, step, 0)

    for q in range(Q):
        m = MC[:, 128 * q : 128 * q + 128]
        top = jnp.max(m, axis=0, keepdims=True)
        total = jnp.sum(SC[:, 128 * q : 128 * q + 128] * jnp.exp2(m - top), axis=0, keepdims=True)
        LC[q : q + 1, :] = top + jnp.log2(total)

    def share_copy(axis, src, dst, me, base, k):
        return rcopy(src, dst.at[me], st_s.at[base + k], st_r.at[base + k], near(axis, k))

    def all_share(axis, n, src, dst, me, base):
        dst[me] = src[...]
        for k in range(1, n):
            start(share_copy, axis, src, dst, me, base, k)
        return [share_copy(axis, src, dst, me, base, k) for k in range(1, n)]

    def arrive(copies):
        for copy in copies:
            copy.wait_recv()

    sx = all_share("f", X, LC, xr_stat, f, 0)

    def lane_combine(b, carry):
        at = pl.ds(pl.multiple_of(128 * b, 128), 128)
        m = MR[at, :].T
        top = jnp.max(m, axis=0, keepdims=True)
        total = jnp.sum(SR[at, :].T * jnp.exp2(m - top), axis=0, keepdims=True)
        LR[pl.ds(b, 1), :] = top + jnp.log2(total)
        return carry

    lax.fori_loop(0, NB, lane_combine, 0)
    sz = all_share("z", Z, LR, zr_stat, z, 16)
    arrive(sx)
    LY[...] = combine(xr_stat[...])
    sy = all_share("g", X, LY, yr_stat, g, 8)

    def transpose_states(b, carry):
        St[:, pl.ds(pl.multiple_of(128 * b, 128), 128)] = S[b // Z, lax.rem(b, Z)].T
        return carry

    lax.fori_loop(0, NB, transpose_states, 0)

    arrive(sz)
    LS[...] = combine(zr_stat[...])
    def ls_copy():
        return rcopy(LS, sib_stat, st_s.at[0], st_r.at[0], sibling)

    start(ls_copy)
    arrive(sy)
    col_lse = combine(yr_stat[...])
    LC2 = col_lse + 1.0
    ls_copy().wait_recv()
    pair = jnp.stack([LS[...], sib_stat[...]])
    row_lse = combine(pair)
    LY2 = row_lse + 1.0
    zr_stat[0] = LY2

    xr_stat[0] = LC2
    loss_s[0] = ((row_lse + col_lse)[:8] + (row_lse + col_lse)[8:]) * (1.0 / NB)
    acc[...] = jnp.zeros(acc.shape, jnp.float32)

    def weights(ff, b, out_ref, n):
        hit_sum = acc[...]
        marks = []
        tops = []
        for j in range(X):
            q = X * ff + j
            marks.append((256 * (c * q + (1 - c) * (X * j + ff))).astype(jnp.float32))
            tops.append(xr_stat[0, pl.ds(q, 1), :])
        for i in range(8):
            at = pl.ds(pl.multiple_of(128 * b + 32 * i, 32), 32)
            rl = MR[at, :]
            pb = PB[at, :]
            for j in range(X):
                l = L[at, pl.ds(pl.multiple_of(512 * ff + 128 * j, 128), 128)]
                prob = jnp.exp2(l - rl) + jnp.exp2(l - tops[j])
                hit = pb == marks[j]
                hit_sum = hit_sum + jnp.sum(jnp.where(hit, l, 0.0).reshape(4, 8, 128), axis=0)
                out_ref[n, at, 128 * j : 128 * j + 128] = jnp.where(hit, prob - 1.0, prob).astype(jnp.bfloat16)
        acc[...] = hit_sum

    def halves(out):
        return [[out[256 * u + 64 * i : 256 * u + 64 * i + 64, :] for i in range(4)] for u in (0, 1)]

    def p1_copy(k, h):
        i = 2 * (k - 1) + h
        return rcopy(
            s1.at[k, pl.ds(2 * h, 2)], r1.at[k - 1, pl.ds(2 * h, 2)], g1_s.at[i], g1_r.at[i], near("f", k)
        )

    def goal_dot(k, h, w_ref, n, u):
        cols = pl.ds(pl.multiple_of(256 * h, 256), 256)
        out = jnp.dot(St[256 * u : 256 * u + 256, :], w_ref[n, :, cols], preferred_element_type=jnp.float32)
        for j in (0, 1):
            GG[X * wrap(f + k, X) + 2 * h + j, 256 * u : 256 * u + 256, :] = out[:, 128 * j : 128 * j + 128]
        return [
            ([out[64 * i : 64 * i + 64, 128 * j : 128 * j + 128] for i in range(4)], s1.at[k, 2 * h + j, u])
            for j in (0, 1)
        ]

    def spread_rows(b, carry):
        at = pl.ds(pl.multiple_of(128 * b, 128), 128)
        MR[at, :] = jnp.broadcast_to(zr_stat[0, pl.ds(b, 1), :], (128, 128)).T
        return carry

    lax.fori_loop(0, NB, spread_rows, 0)
    order = (2, 1, 3, 0)
    W = (W0, W1)

    def chunk_block(n, mine):
        pair = lax.rem(z // 2 + H // 2 + jnp.right_shift(156, 2 * n), H)
        return (c + (1 - mine) * (1 - 2 * c)) * Z + 2 * pair

    def state_term(b, m, out):
        rows = pl.ds(pl.multiple_of(128 * b, 256), 256)
        term = jnp.dot(
            W[m % 2][m // 2, rows, :],
            G[pl.ds(X * wrap(f + order[m], X), X)].reshape(512, E),
            preferred_element_type=jnp.float32,
        )
        return term if out is None else out + term

    def state_part(n, mine):
        b = chunk_block(n, mine)
        out = None
        for m in range(X):
            out = state_term(b, m, out)
        GS[pl.ds(b, 2)] = out.reshape(2, 128, E)

    def rb_copy(n):
        b = chunk_block(n, 0)
        pair = lax.rem(b, Z) // 2
        return rcopy(GS.at[pl.ds(b, 2)], GR.at[pl.ds(2 * pair, 2)], rb_s.at[n], rb_r.at[n], sibling)

    def rz_copy(s, u, k):
        sg = 0 if s > 0 else 1
        i = (sg * 2 + u) * H + k - 1
        return rcopy(zs.at[i], zr.at[i], rz_s.at[i], rz_r.at[i], near("z", s))

    def gs_slabs(zz, u):
        rows = pl.ds(64 * u, 64)
        return [
            GS[c * Z + zz, rows, 128 * i : 128 * i + 128] + GR[zz, rows, 128 * i : 128 * i + 128]
            for i in range(4)
        ]

    def z_step(k, lead):
        items = [(s, u) for s in signs for u in (0, 1) if lead == (u == (s < 0))]
        last = k == (H if lead else H - 1)
        ready = []
        for s, u in items:
            at = ((0 if s > 0 else 1) * 2 + u) * H + k
            slabs = gs_slabs(wrap(z + s * k, Z), u)
            if not last:
                rz_copy(s, u, k + 1).wait_recv()
                slabs = [a + b for a, b in zip(slabs, restore(zr.at[at]))]
            ready.append((slabs, zs.at[at - 1]))
        quantize_all(ready)
        for s, u in items:
            rz_copy(s, u, k).start()

    def loss_copy(stage, k):
        i = (0, 0, 4, 8)[stage] + k
        to = sibling if stage == 0 else near(" fgz"[stage], k)
        return rcopy(loss_s.at[stage], loss_r.at[i], st_s.at[32 + i], st_r.at[32 + i], to)

    loss_peers = ((0,), range(1, X), range(1, X), range(1, Z))

    def loss_share(stage):
        for k in loss_peers[stage]:
            start(loss_copy, stage, k)

    def loss_add(stage):
        total = loss_s[stage]
        for k in loss_peers[stage]:
            loss_copy(stage, k).wait_recv()
            total = total + loss_r[(0, 0, 4, 8)[stage] + k]
        return total

    def part_and_give(n, carry):
        state_part(n, 0)
        rb_copy(n).start()
        return carry

    def part_only(n, carry):
        state_part(n, 1)
        return carry

    first = [chunk_block(0, mine) for mine in (0, 1)]
    for m in range(X):
        weights(wrap(f + order[m], X), first[0], W[m % 2], m // 2)
    out = None
    for m in range(X):
        out = state_term(first[0], m, out)
        weights(wrap(f + order[m], X), first[1], W[m % 2], m // 2)
    GS[pl.ds(first[0], 2)] = out.reshape(2, 128, E)
    rb_copy(0).start()
    state_part(0, 1)

    def group(n):
        def half(r, carry):
            for i in (1, 2, 3):
                weights(wrap(f + order[n], X), chunk_block(i, r), W[n % 2], n // 2)
            return carry

        lax.fori_loop(0, 2, half, 0)

    def goals(n):
        def half(h, carry):
            ready = goal_dot(order[n], h, W[n % 2], n // 2, 0)
            ready += goal_dot(order[n], h, W[n % 2], n // 2, 1)
            if order[n] > 0:
                quantize_all(ready)
                p1_copy(order[n], h).start()
            return carry

        lax.fori_loop(0, 2, half, 0)

    for n in range(X):
        group(n)
        if n < X - 1:
            goals(n)
        if n == 0:
            rb_copy(0).wait_recv()
            z_step(H, True)
    loss_s[0] = loss_s[0] - 2.0 * acc[...]
    loss_share(0)
    lax.fori_loop(1, 3, part_and_give, 0)
    loss_s[1] = loss_add(0)
    loss_share(1)
    lax.fori_loop(1, 3, part_only, 0)
    for n in (1, 2):
        rb_copy(n).wait_recv()
    z_step(H - 1, True)
    z_step(H - 1, False)
    lax.fori_loop(3, 4, part_and_give, 0)
    lax.fori_loop(3, 4, part_only, 0)
    goals(X - 1)
    rb_copy(3).wait_recv()
    loss_s[2] = loss_add(1)
    loss_share(2)
    z_step(H - 2, True)
    z_step(H - 2, False)

    def p2_copy(k):
        return rcopy(s2.at[k - 1], r2.at[k - 1], g2_s.at[k - 1], g2_r.at[k - 1], near("g", k))

    def summed(gg):
        blocks = halves(GG[X * f + gg])
        for k in (2, 1, 3):
            for u in (0, 1):
                blocks[u] = [a + b for a, b in zip(blocks[u], restore(r1.at[k - 1, gg, u]))]
        return blocks

    for k in (2, 1, 3):
        for h in (0, 1):
            p1_copy(k, h).wait_recv()
    for k in (2, 1, 3):
        quantize_all([(slabs, s2.at[k - 1, u]) for u, slabs in enumerate(summed(wrap(g + k, X)))])
        p2_copy(k).start()
    loss_s[3] = loss_add(2)
    loss_share(3)
    z_step(1, True)
    z_step(1, False)
    mine = summed(g)

    for make, args in started:
        make(*args).wait_send()
    for n in range(4):
        rb_copy(n).wait_send()
    for k in range(1, X):
        for h in (0, 1):
            p1_copy(k, h).wait_send()
    for s in signs:
        for u in (0, 1):
            for k in range(2, (H if u == (s < 0) else H - 1) + 1):
                rz_copy(s, u, k).wait_send()

    for k in (1, 3, 2):
        p2_copy(k).wait_recv()
        for u in (0, 1):
            mine[u] = [a + b for a, b in zip(mine[u], restore(r2.at[k - 1, u]))]
    for u in (0, 1):
        for i, part in enumerate(mine[u]):
            GG[home, 256 * u + 64 * i : 256 * u + 64 * i + 64, :] = part
    out_goal[...] = GG[home].T
    gg_store = pltpu.make_async_copy(out_goal, gg_out, in_sem.at[1])
    gg_store.start()
    for u in (0, 1):
        slabs = gs_slabs(z, u)
        for s in signs:
            rz_copy(s, u, 1).wait_recv()
            slabs = [a + b for a, b in zip(slabs, restore(zr.at[((0 if s > 0 else 1) * 2 + u) * H]))]
        for i, part in enumerate(slabs):
            GS[c * Z + z, 64 * u : 64 * u + 64, 128 * i : 128 * i + 128] = part
    gs_store = pltpu.make_async_copy(GS.at[c * Z + z], gs_out, in_sem.at[0])
    gs_store.start()
    total = loss_add(3)
    loss_out[0, 0] = jnp.sum(total) * (LN2 / (4.0 * Q * Z * B))

    for k in range(1, X):
        p2_copy(k).wait_send()
    for s in signs:
        for u in (0, 1):
            rz_copy(s, u, 1).wait_send()
    gs_store.wait()
    gg_store.wait()


def hand_over(gs_in, gg_in, loss_in, gs_out, gg_out, loss_out):
    gs_out[...] = gs_in[...]
    gg_out[...] = gg_in[...]
    loss_out[0, 0] = loss_in[0, 0]


def body(state_emb, goal_emb, positive):
    Z = lax.axis_size("gl")
    H = Z // 2
    NB = 2 * Z
    R, C = NB * B, Q * B
    vmem = pltpu.VMEM
    f32, bf16, i16 = jnp.float32, jnp.bfloat16, jnp.int16
    dma = pltpu.SemaphoreType.DMA
    scratch = [
        vmem((2, Z, B, E), bf16), vmem((Q, B, E), bf16), vmem((2, Z, B), jnp.int32),
        vmem((R, C), f32), vmem((2, R, C // 4), bf16), vmem((2, R, C // 4), bf16), vmem((E, R), bf16),
        vmem((NB, B, E), f32), vmem((Z, B, E), f32), vmem((Q, E, B), f32),
        vmem((R, B), f32), vmem((R, B), f32), vmem((R, B), f32), vmem((8, C), f32), vmem((8, C), f32),
        vmem((NB, B), f32), vmem((Z, NB, B), f32), vmem((NB, B), f32), vmem((NB, B), f32),
        vmem((Q, B), f32), vmem((X, Q, B), f32), vmem((Q, B), f32), vmem((X, Q, B), f32),
        vmem((8, B), f32),
        vmem((4 * H, UNIT, B), i16), vmem((4 * H, UNIT, B), i16),
        vmem((X, X, 2, UNIT, B), i16), vmem((X - 1, X, 2, UNIT, B), i16),
        vmem((X - 1, 2, UNIT, B), i16), vmem((X - 1, 2, UNIT, B), i16),
        vmem((4, 8, B), f32), vmem((8 + Z, 8, B), f32), vmem((B, E), f32),
        dma((3,)), dma((4 * H,)), dma((4 * H,)), dma((3,)), dma((3,)), dma((12,)), dma((12,)),
        dma((Z + 1,)), dma((Z + 1,)), dma((48,)), dma((48,)), dma((4,)), dma((4,)),
        dma((4 * H,)), dma((4 * H,)), dma((6,)), dma((6,)), dma((3,)), dma((3,)),
    ]
    there = pl.BlockSpec(memory_space=pl.ANY)
    whole = pl.BlockSpec(memory_space=pltpu.VMEM)
    scalar = pl.BlockSpec(memory_space=pltpu.SMEM)
    shapes = (
        jax.ShapeDtypeStruct((B, E), f32),
        jax.ShapeDtypeStruct((B, E), f32),
        jax.ShapeDtypeStruct((1, 1), f32),
    )
    results = pl.pallas_call(
        functools.partial(kernel, Z),
        out_shape=shapes,
        in_specs=[there] * 3,
        out_specs=(there, there, scalar),
        scratch_shapes=scratch,
        compiler_params=pltpu.CompilerParams(
            collective_id=0, has_side_effects=True, vmem_limit_bytes=62 * 1024 * 1024
        ),
    )(state_emb, goal_emb, positive.reshape(Z, B))
    grad_state, grad_goal, loss = pl.pallas_call(
        hand_over,
        out_shape=shapes,
        in_specs=[whole, whole, scalar],
        out_specs=(whole, whole, scalar),
    )(*results)
    return grad_state, grad_goal, loss.reshape(())


def solution(mesh):
    return jax.shard_map(
        body,
        mesh=mesh,
        in_specs=(P(("st", "gl"), None), P(("gl", "st"), None), P("st")),
        out_specs=(P(("st", "gl"), None), P(("gl", "st"), None), P()),
        check_vma=False,
    )
```
